128 devices in a mesh: dp: 8 (over y, z_lo), seq: 16 (over z_hi, x, core).
Axes of the slice: x: 4, y: 4, z: 4 (z_hi: 2, z_lo: 2; z = z_hi * 2 + z_lo), core: 2. Of those that a mesh axis runs over, the one named last changes fastest.
Arguments:
- query: bfloat16 [8, 12288, 1536], P('dp', 'seq'), may hold values from -6 to 6
- key_states: bfloat16 [8, 12288, 1536], P('dp', 'seq'), may hold values from -6 to 6
- value_states: bfloat16 [8, 12288, 1536], P('dp', 'seq'), may hold values from -6 to 6
- attn_out: bfloat16 [8, 12288, 1536], P('dp', 'seq'), may hold values from -0.59765625 to 0.59765625
- log_norm: float32 [8, 12, 12288], P('dp', None, 'seq'), may hold values from 6 to 7
- out_grad: bfloat16 [8, 12288, 3072], P('dp', 'seq'), may hold values from -24 to 24
- out_weight: bfloat16 [1536, 3072], P('dp'), may hold values from -0.15625 to 0.15625
- tile_lists: int32 [8, 32, 3], P('dp'), may hold values from 0 to 31, as said below
Outputs:
- query_grad: bfloat16 [8, 12288, 1536], P('dp', 'seq')
- key_grad: bfloat16 [8, 12288, 1536], P('dp', 'seq')
- value_grad: bfloat16 [8, 12288, 1536], P('dp', 'seq')
- weight_grad: float32 [1536, 3072], P('dp')
The draws below stay inside these ranges and needn't reach their ends.
Inputs may be any that keep to these rules, and one draw needn't show every extreme that they name: `tile_lists`: row i of a clip's list names 3 different tiles: tile i itself and tiles j with (i // 2) * 2 - 1 <= j <= (i // 2) * 2 + 2.
All inputs are finite; a program needn't handle non-finite values.
Results may differ from the reference program's by a relative error of at most 0.0095.
Values may be sent and summed in bfloat16 or wider, within the bound.
No kernel may reach another device: no remote copies, remote signals or barrier semaphores. Data moves between devices by JAX's collectives and lax.ppermute only.
A program may use at most 256 MiB of HBM per device.

```python
import math
import jax
import jax.numpy as jnp
from jax import lax

D = 3072
HEADS = 12
HD = 128
TILE = 384
KEEP = 3
TPD = 2
TOK_DEV = 768
CLIP_TOK = 12288
CLIP_TILES = 32
CLIPS = 8
HH = 1536
N_SEQ = 16


def draw_tile_lists(key, part):
    span = TPD + 2
    tile_index = jnp.arange(CLIP_TILES, dtype=jnp.int32)
    tile_slab = tile_index // TPD
    candidate = jnp.arange(span, dtype=jnp.int32)
    candidate_tile = tile_slab[:, None] * TPD - 1 + candidate[None, :]
    in_range = (candidate_tile >= 0) & (candidate_tile < CLIP_TILES)
    is_self = candidate_tile == tile_index[:, None]
    random_bits = jax.random.randint(key, (CLIPS, CLIP_TILES, span), 0, 1 << 20, dtype=jnp.int32)
    priority = random_bits * 64 + candidate[None, None, :]
    priority = jnp.where(is_self[None], jnp.int32(1 << 27), jnp.where(in_range[None], priority, jnp.int32(-1)))
    chosen = lax.top_k(priority, KEEP)[1]
    full_tiles = jnp.broadcast_to(candidate_tile[None], (CLIPS, CLIP_TILES, span))
    return jnp.take_along_axis(full_tiles, chosen, axis=2).astype(jnp.int32)


def steps_of(stream_key, dims, shards, low, top_value):
    def one(axis_at, parts):
        heights = jax.random.uniform(jax.random.fold_in(jax.random.fold_in(stream_key, 6), axis_at), (parts,), jnp.float32, low / len(shards), top_value / len(shards))
        return jnp.repeat(jnp.exp(heights), dims[axis_at] // parts).reshape((-1,) + (1,) * (len(dims) - axis_at - 1))

    level = one(*shards[0])
    for cut in shards[1:]:
        level = level * one(*cut)
    return level


def bell_draw(stream_key, extent, scale, most, cuts=(), kind=jnp.bfloat16):
    array = scale * jax.random.normal(stream_key, extent, jnp.float32)
    if cuts:
        array = array * steps_of(stream_key, extent, cuts, -0.22, 0.18)
    return jnp.clip(array, -most, most).astype(kind)


def setup_inputs(seed: int = 0) -> dict:
    streams_of = jax.random.split(jax.random.key(seed), 9)
    return {
        "query": bell_draw(streams_of[0], (CLIPS, CLIP_TOK, HH), 1.0, 6.0, ((0, 8), (1, 16))),
        "key_states": bell_draw(streams_of[1], (CLIPS, CLIP_TOK, HH), 1.0, 6.0, ((0, 8), (1, 16))),
        "value_states": bell_draw(streams_of[2], (CLIPS, CLIP_TOK, HH), 1.0, 6.0, ((0, 8), (1, 16))),
        "attn_out": bell_draw(streams_of[3], (CLIPS, CLIP_TOK, HH), 0.1, 0.59765625, ((0, 8), (1, 16))),
        "log_norm": jnp.clip(6.0 + 1.0 * jax.random.uniform(streams_of[4], (CLIPS, HEADS, CLIP_TOK), jnp.float32) ** steps_of(streams_of[4], (CLIPS, HEADS, CLIP_TOK), ((0, 8), (2, 16)), -0.2, 0.2), 6.0, 7.0),
        "out_grad": bell_draw(streams_of[5], (CLIPS, CLIP_TOK, D), 4.0, 24.0, ((0, 8), (1, 16))),
        "out_weight": bell_draw(streams_of[6], (HH, D), HH ** -0.5, 0.15625, ((0, 8),)),
        "tile_lists": draw_tile_lists(jax.random.fold_in(streams_of[8], 71), 0),
    }


def slab_terms(query, key_pad, value_pad, attn_grad, log_norm, row_delta, tile_lists, slab_index):
    score_scale = 1.0 / math.sqrt(HD)
    window_rows = TOK_DEV + 2 * TILE
    row_start = (slab_index * TOK_DEV).astype(jnp.int32)
    q_rows = lax.dynamic_slice_in_dim(query, row_start, TOK_DEV, 0).astype(jnp.float32).reshape(TOK_DEV, HEADS, HD)
    g_rows = lax.dynamic_slice_in_dim(attn_grad, row_start, TOK_DEV, 0).astype(jnp.float32).reshape(TOK_DEV, HEADS, HD)
    norm_rows = lax.dynamic_slice_in_dim(log_norm, row_start, TOK_DEV, 1)
    delta_rows = lax.dynamic_slice_in_dim(row_delta, row_start, TOK_DEV, 1)
    key_window = lax.dynamic_slice_in_dim(key_pad, row_start, window_rows, 0).astype(jnp.float32).reshape(window_rows, HEADS, HD)
    value_window = lax.dynamic_slice_in_dim(value_pad, row_start, window_rows, 0).astype(jnp.float32).reshape(window_rows, HEADS, HD)
    slab_lists = lax.dynamic_slice_in_dim(tile_lists, (slab_index * TPD).astype(jnp.int32), TPD, 0)
    window_ids = (slab_index * TPD - 1).astype(jnp.int32) + jnp.arange(TPD + 2, dtype=jnp.int32)
    tile_mask = jnp.any(slab_lists[:, :, None] == window_ids[None, None, :], axis=1)
    token_mask = jnp.repeat(jnp.repeat(tile_mask, TILE, axis=0), TILE, axis=1)
    scores = jnp.einsum('qhd,khd->hqk', q_rows, key_window) * score_scale
    weights = jnp.where(token_mask[None], jnp.exp(scores - norm_rows[:, :, None]), 0.0)
    weights_half = lax.optimization_barrier(weights.astype(jnp.bfloat16)).astype(jnp.float32)
    prob_grad = jnp.einsum('qhd,khd->hqk', g_rows, value_window)
    score_grad = lax.optimization_barrier((weights * (prob_grad - delta_rows[:, :, None])).astype(jnp.bfloat16)).astype(jnp.float32)
    query_part = jnp.einsum('hqk,khd->qhd', score_grad, key_window) * score_scale
    key_part = jnp.einsum('hqk,qhd->khd', score_grad, q_rows)
    value_part = jnp.einsum('hqk,qhd->khd', weights_half, g_rows)
    return (query_part.reshape(TOK_DEV, HH), key_part.reshape(window_rows, HH), value_part.reshape(window_rows, HH))

def clip_grads(query, key_states, value_states, attn_grad, log_norm, row_delta, tile_lists):
    padding = ((TILE, TILE), (0, 0))
    key_pad = jnp.pad(key_states, padding)
    value_pad = jnp.pad(value_states, padding)
    window_rows = TOK_DEV + 2 * TILE
    empty_acc = jnp.zeros((CLIP_TOK + 2 * TILE, HH), jnp.float32)
    window_row = jnp.arange(window_rows, dtype=jnp.int32)
    is_rim = ((window_row < TILE) | (window_row >= TILE + TOK_DEV))[:, None]

    def cross_round(part):
        rounded = lax.optimization_barrier(part.astype(jnp.bfloat16)).astype(jnp.float32)
        return jnp.where(is_rim, rounded, part)

    def slab_step(totals, slab_index):
        key_acc, value_acc = totals
        query_part, key_part, value_part = slab_terms(query, key_pad, value_pad, attn_grad, log_norm, row_delta, tile_lists, slab_index)
        key_part = cross_round(key_part)
        value_part = cross_round(value_part)
        row_start = (slab_index * TOK_DEV).astype(jnp.int32)
        key_acc = lax.dynamic_update_slice_in_dim(key_acc, lax.dynamic_slice_in_dim(key_acc, row_start, window_rows, 0) + key_part, row_start, 0)
        value_acc = lax.dynamic_update_slice_in_dim(value_acc, lax.dynamic_slice_in_dim(value_acc, row_start, window_rows, 0) + value_part, row_start, 0)
        return ((key_acc, value_acc), query_part.astype(jnp.bfloat16))
    (key_acc, value_acc), query_rows = lax.scan(slab_step, (empty_acc, empty_acc), jnp.arange(N_SEQ, dtype=jnp.int32))
    score_scale = 1.0 / math.sqrt(HD)
    query_grad = query_rows.reshape(CLIP_TOK, HH)
    key_grad = (key_acc[TILE:TILE + CLIP_TOK] * score_scale).astype(jnp.bfloat16)
    value_grad = value_acc[TILE:TILE + CLIP_TOK].astype(jnp.bfloat16)
    return (query_grad, key_grad, value_grad)

def reference(query, key_states, value_states, attn_out, log_norm, out_grad, out_weight, tile_lists):
    flat_out = attn_out.reshape(CLIPS * CLIP_TOK, HH)
    flat_grad = out_grad.reshape(CLIPS * CLIP_TOK, D)
    weight_grad = jnp.dot(flat_out.T, flat_grad, preferred_element_type=jnp.float32)
    attn_grad = jnp.dot(flat_grad, out_weight.T, preferred_element_type=jnp.float32).astype(jnp.bfloat16)
    row_delta = (attn_grad.astype(jnp.float32) * flat_out.astype(jnp.float32)).reshape(CLIPS, CLIP_TOK, HEADS, HD).sum(axis=3)
    row_delta = jnp.transpose(row_delta, (0, 2, 1))
    attn_grad = attn_grad.reshape(CLIPS, CLIP_TOK, HH)

    def one_clip(clip_items):
        return clip_grads(*clip_items)
    query_grad, key_grad, value_grad = lax.map(one_clip, (query, key_states, value_states, attn_grad, log_norm, row_delta, tile_lists))
    return (query_grad, key_grad, value_grad, weight_grad)
```

```python
import functools
import math

import jax
import jax.numpy as jnp
from jax import lax
from jax.experimental import pallas as pl
from jax.experimental.pallas import tpu as pltpu
from jax.sharding import PartitionSpec as P

TILE = 384
HEAD = 128
LOG2E = math.log2(math.e)
SCALE = 1.0 / math.sqrt(HEAD)
F32 = jnp.float32
BF16 = jnp.bfloat16
NT = (((1,), (1,)), ((), ()))
NN = (((1,), (0,)), ((), ()))
TN = (((0,), (0,)), ((), ()))


def dot(a, b, dims):
    return lax.dot_general(a, b, dims, preferred_element_type=F32)


def attend_kernel(
    meta, q, kb, ko, ka, vb, vo, va, g, o, norm, dq_in, dq, dko, dvo, low, high, kw, vw, dka, dva
):
    head = meta[6] + pl.program_id(0)
    kw[0] = kb[...]
    kw[1] = ko[:TILE]
    kw[2] = ko[TILE:]
    kw[3] = ka[...]
    vw[0] = vb[...]
    vw[1] = vo[:TILE]
    vw[2] = vo[TILE:]
    vw[3] = va[...]
    dka[...] = jnp.zeros_like(dka)
    dva[...] = jnp.zeros_like(dva)
    ones = jnp.ones((16, HEAD), BF16)
    for t in range(2):
        rows = slice(t * TILE, (t + 1) * TILE)
        qt = q[rows, :]
        gt = g[rows, :]
        prod = gt.astype(F32) * o[rows, :].astype(F32)
        coarse = prod.astype(BF16)
        fine = (prod - coarse.astype(F32)).astype(BF16)
        delta = (dot(ones, coarse, NT) + dot(ones, fine, NT))[0:1]
        shift = norm[pl.ds(head, 1), rows] * LOG2E
        total = None
        for j in range(3):
            slot = meta[t * 3 + j]
            k = kw[slot]
            weights = jnp.exp2(dot(k, qt, NT) * (SCALE * LOG2E) - shift)
            score_grad = (weights * (dot(vw[slot], gt, NT) - delta)).astype(BF16)
            dva[slot] += dot(weights.astype(BF16), gt, NN)
            dka[slot] += dot(score_grad, qt, NN)
            part = dot(k, score_grad, TN)
            total = part if total is None else total + part
        dq[rows, :] = (total * SCALE).T.astype(BF16)
    dko[...] = dka[1:3].reshape(2 * TILE, HEAD)
    dvo[...] = dva[1:3].reshape(2 * TILE, HEAD)
    low[0] = dka[0].astype(BF16)
    low[1] = dva[0].astype(BF16)
    high[0] = dka[3].astype(BF16)
    high[1] = dva[3].astype(BF16)


def attend(meta, q, kb, ko, ka, vb, vo, va, g, o, norm, dq_full):
    heads = g.shape[1] // HEAD
    own = pl.BlockSpec((2 * TILE, HEAD), lambda i, m: (0, i + m[6]))
    rim = pl.BlockSpec((TILE, HEAD), lambda i, m: (0, i + m[6]))
    local = pl.BlockSpec((2 * TILE, HEAD), lambda i, m: (0, i))
    local_rim = pl.BlockSpec((2, TILE, HEAD), lambda i, m: (0, 0, i))
    whole = pl.BlockSpec(norm.shape, lambda i, m: (0, 0))
    anywhere = pl.BlockSpec(memory_space=pl.ANY)
    wide = jax.ShapeDtypeStruct((2 * TILE, heads * HEAD), F32)
    rims = jax.ShapeDtypeStruct((2, TILE, heads * HEAD), BF16)
    flops = heads * 6 * 5 * 2 * TILE * TILE * HEAD
    return pl.pallas_call(
        attend_kernel,
        grid_spec=pltpu.PrefetchScalarGridSpec(
            num_scalar_prefetch=1,
            grid=(heads,),
            in_specs=[own, rim, own, rim, rim, own, rim, local, own, whole, anywhere],
            out_specs=[own, local, local, local_rim, local_rim],
            scratch_shapes=[
                pltpu.VMEM((4, TILE, HEAD), BF16),
                pltpu.VMEM((4, TILE, HEAD), BF16),
                pltpu.VMEM((4, TILE, HEAD), F32),
                pltpu.VMEM((4, TILE, HEAD), F32),
            ],
        ),
        out_shape=[jax.ShapeDtypeStruct(q.shape, BF16), wide, wide, rims, rims],
        input_output_aliases={11: 0},
        compiler_params=pltpu.CompilerParams(vmem_limit_bytes=32 << 20),
        cost_estimate=pl.CostEstimate(
            flops=3 * flops, bytes_accessed=heads * 3_000_000, transcendentals=heads * 6 * TILE * TILE
        ),
    )(meta, q, kb, ko, ka, vb, vo, va, g, o, norm, dq_full)


def combine_kernel(meta, dko, dvo, below, above, dk_in, dv_in, dk, dv):
    dk[:TILE] = ((dko[:TILE] + below[0].astype(F32)) * SCALE).astype(BF16)
    dk[TILE:] = ((dko[TILE:] + above[0].astype(F32)) * SCALE).astype(BF16)
    dv[:TILE] = (dvo[:TILE] + below[1].astype(F32)).astype(BF16)
    dv[TILE:] = (dvo[TILE:] + above[1].astype(F32)).astype(BF16)


def combine(meta, dko, dvo, below, above, dk_full, dv_full):
    width = dko.shape[1]
    own = pl.BlockSpec((2 * TILE, HEAD), lambda i, m: (0, i))
    rim = pl.BlockSpec((2, TILE, HEAD), lambda i, m: (0, 0, i))
    placed = pl.BlockSpec((2 * TILE, HEAD), lambda i, m: (0, i + m[6]))
    anywhere = pl.BlockSpec(memory_space=pl.ANY)
    full = jax.ShapeDtypeStruct(dk_full.shape, BF16)
    return pl.pallas_call(
        combine_kernel,
        grid_spec=pltpu.PrefetchScalarGridSpec(
            num_scalar_prefetch=1,
            grid=(width // HEAD,),
            in_specs=[own, own, rim, rim, anywhere, anywhere],
            out_specs=[placed, placed],
        ),
        out_shape=[full, full],
        input_output_aliases={5: 0, 6: 1},
        compiler_params=pltpu.CompilerParams(vmem_limit_bytes=16 << 20),
        cost_estimate=pl.CostEstimate(flops=4_000_000, bytes_accessed=8_000_000, transcendentals=0),
    )(meta, dko, dvo, below, above, dk_full, dv_full)


def body(query, key_states, value_states, attn_out, log_norm, out_grad, out_weight, tile_lists):
    grad_rows = out_grad[0]
    out_rows = attn_out[0]
    q, k, v = query[0], key_states[0], value_states[0]
    norm = log_norm[0]
    tokens, width = q.shape
    model = grad_rows.shape[1]
    n_dp = lax.axis_size("dp")
    n_seq = lax.axis_size("seq")
    dp = lax.axis_index("dp")
    seq = lax.axis_index("seq")
    y = dp // 2
    core = seq % 2
    n_y = n_dp // 2

    def over_dp(value, target):
        return lax.ppermute(value, "dp", [(i, target(i)) for i in range(n_dp)])

    def over_seq(value, target):
        pairs = [(i, target(i)) for i in range(n_seq)]
        return lax.ppermute(value, "seq", [(i, j) for i, j in pairs if 0 <= j < n_seq])

    def swap(value):
        return over_seq(value, lambda i: i ^ 1)

    def flip(value):
        return over_dp(value, lambda i: i ^ 1)

    def up(value):
        return over_dp(value, lambda i: (i + 2) % n_dp)

    def down(value):
        return over_dp(value, lambda i: (i - 2) % n_dp)

    def take(value, index):
        return lax.dynamic_index_in_dim(value, index, 0, keepdims=False)

    half = model // 2
    mine = lax.dynamic_slice_in_dim(out_weight, core * half, half, 1)
    other = flip(mine)
    low_first = dp % 2 == 0
    pair0 = jnp.concatenate(
        [jnp.where(low_first, mine, other), jnp.where(low_first, other, mine)], axis=0
    )
    k_before = over_seq(k[tokens - TILE :], lambda i: i + 1)
    v_before = over_seq(v[tokens - TILE :], lambda i: i + 1)
    k_after = over_seq(k[:TILE], lambda i: i - 1)
    v_after = over_seq(v[:TILE], lambda i: i - 1)
    from_up = down(pair0)
    from_down = up(pair0)
    rows = pair0.shape[0]
    far_low = up(from_down[: rows // 2])
    far_high = down(from_up[rows // 2 :])
    slabs = [pair0, from_up, from_down, jnp.concatenate([far_low, far_high], axis=0)]
    groups = [y, (y + 1) % n_y, (y + n_y - 1) % n_y, (y + 2) % n_y]

    first_tile = seq * 2 - 1
    slots = (lax.dynamic_slice_in_dim(tile_lists[0], seq * 2, 2, 0) - first_tile).reshape(-1)

    send_grad = lax.dynamic_slice_in_dim(grad_rows, (1 - core) * half, half, 1)
    keep_grad = lax.dynamic_slice_in_dim(grad_rows, core * half, half, 1)
    sent = swap(dot(out_rows, send_grad, TN).astype(BF16))
    kept = dot(out_rows, keep_grad, TN)
    chip_sum = (kept + sent.astype(F32)).astype(BF16).reshape(n_y, width // n_y, half)

    group_heads = width // n_y // HEAD
    dq = jnp.zeros((tokens, width), BF16)
    dk = jnp.zeros((tokens, width), BF16)
    dv = jnp.zeros((tokens, width), BF16)
    pending = []
    for slab, group in zip(slabs, groups):
        across = swap(slab)
        rows_here = jnp.concatenate(
            [jnp.where(core == 0, slab, across), jnp.where(core == 0, across, slab)], axis=1
        )
        g = dot(grad_rows, rows_here, NT).astype(BF16)
        meta = jnp.concatenate([slots, (group * group_heads)[None]]).astype(jnp.int32)
        dq, dko, dvo, low, high = attend(
            meta, q, k_before, k, k_after, v_before, v, v_after, g, out_rows, norm, dq
        )
        below = over_seq(high, lambda i: i + 1)
        above = over_seq(low, lambda i: i - 1)
        pending.append((meta, dko, dvo, below, above))

    quarter = width // n_y
    far = take(chip_sum, (y + 2) % n_y)
    add_low = up(far[: quarter // 2])
    add_high = down(far[quarter // 2 :])
    plus = take(chip_sum, (y + 1) % n_y)
    minus = take(chip_sum, (y + n_y - 1) % n_y)
    plus = jnp.concatenate(
        [(plus[: quarter // 2].astype(F32) + add_low.astype(F32)).astype(BF16), plus[quarter // 2 :]]
    )
    minus = jnp.concatenate(
        [minus[: quarter // 2], (minus[quarter // 2 :].astype(F32) + add_high.astype(F32)).astype(BF16)]
    )
    from_minus = up(plus)
    from_plus = down(minus)
    y_sum = take(chip_sum, y).astype(F32) + from_minus.astype(F32) + from_plus.astype(F32)
    y_sum = y_sum.reshape(2, quarter // 2, half)
    passed = flip(take(y_sum, 1 - dp % 2).astype(BF16))
    dp_sum = take(y_sum, dp % 2) + passed.astype(F32)
    x = (seq // 2) % 4
    n_x = 4
    piece = dp_sum.shape[0] // n_x

    def shift_x(i, by):
        return i // 8 * 8 + ((i // 2 + by) % n_x) * 2 + i % 2

    parts = dp_sum.reshape(n_x, piece, half)
    total = take(parts, x)
    for by in range(1, n_x):
        out = take(parts, (x + by) % n_x).astype(BF16)
        total = total + over_seq(out, lambda i, by=by: shift_x(i, by)).astype(F32)
    crossed = over_seq(total.astype(BF16), lambda i: (i + 8) % 16)
    total = (total.astype(BF16).astype(F32) + crossed.astype(F32)).astype(BF16)
    ready = jnp.zeros((n_x, piece, half), BF16)
    ready = lax.dynamic_update_index_in_dim(ready, total, x, 0)
    for by in range(1, n_x):
        got = over_seq(total, lambda i, by=by: shift_x(i, by))
        ready = lax.dynamic_update_index_in_dim(ready, got, (x + n_x - by) % n_x, 0)
    ready = ready.reshape(n_x * piece, half)
    partner = swap(ready)
    weight_grad = jnp.concatenate(
        [jnp.where(core == 0, ready, partner), jnp.where(core == 0, partner, ready)], axis=1
    ).astype(F32)

    for item in pending:
        dk, dv = combine(*item, dk, dv)
    return (dq[None], dk[None], dv[None], weight_grad)


def solution(mesh):
    placed = (
        P("dp", "seq", None),
        P("dp", "seq", None),
        P("dp", "seq", None),
        P("dp", "seq", None),
        P("dp", None, "seq"),
        P("dp", "seq", None),
        P("dp", None),
        P("dp", None, None),
    )
    return jax.shard_map(
        body,
        mesh=mesh,
        in_specs=placed,
        out_specs=(P("dp", "seq", None), P("dp", "seq", None), P("dp", "seq", None), P("dp", None)),
        check_vma=False,
    )
```

```python
import functools
import math

import jax
import jax.numpy as jnp
from jax import lax
from jax.experimental import pallas as pl
from jax.experimental.pallas import tpu as pltpu
from jax.sharding import PartitionSpec as P

TILE = 384
HEAD = 128
LOG2E = math.log2(math.e)
SCALE = 1.0 / math.sqrt(HEAD)
F32 = jnp.float32
BF16 = jnp.bfloat16
NT = (((1,), (1,)), ((), ()))
NN = (((1,), (0,)), ((), ()))
TN = (((0,), (0,)), ((), ()))


def dot(a, b, dims):
    return lax.dot_general(a, b, dims, preferred_element_type=F32)


HEADS_AT = 7


def attend_kernel(slabs, *refs):
    meta, q, kb, ko, ka, vb, vo, va, near, away, o, norm = refs[:12]
    weights_in = refs[12 : 12 + 2 * slabs]
    dq, dko, dvo, low, high, kw, vw, dka, dva, gs = refs[13 + 2 * slabs :]
    step = pl.program_id(0)
    head = meta[HEADS_AT + step]
    per = gs.shape[0]
    for n in range(slabs):

        @pl.when(step == n * per)
        def _(n=n):
            made = dot(near[...], weights_in[2 * n][...], NT)
            made += dot(away[...], weights_in[2 * n + 1][...], NT)
            for m in range(per):
                gs[m] = made[:, m * HEAD : (m + 1) * HEAD].astype(BF16)

    g = gs.at[lax.rem(step, per)]
    kw[0] = kb[0]
    kw[1] = ko[:TILE]
    kw[2] = ko[TILE:]
    kw[3] = ka[0]
    vw[0] = vb[0]
    vw[1] = vo[:TILE]
    vw[2] = vo[TILE:]
    vw[3] = va[0]
    dka[...] = jnp.zeros_like(dka)
    dva[...] = jnp.zeros_like(dva)
    ones = jnp.ones((16, HEAD), BF16)
    for t in range(2):
        rows = slice(t * TILE, (t + 1) * TILE)
        qt = q[rows, :]
        gt = g[rows, :]
        prod = gt.astype(F32) * o[rows, :].astype(F32)
        coarse = prod.astype(BF16)
        fine = (prod - coarse.astype(F32)).astype(BF16)
        delta = (dot(ones, coarse, NT) + dot(ones, fine, NT))[0:1]
        shift = norm[pl.ds(head, 1), rows] * LOG2E
        total = None
        for j in range(3):
            slot = meta[t * 3 + j]
            k = kw[slot]
            weights = jnp.exp2(dot(k, qt, NT) * (SCALE * LOG2E) - shift)
            score_grad = (weights * (dot(vw[slot], gt, NT) - delta)).astype(BF16)
            dva[slot] += dot(weights.astype(BF16), gt, NN)
            dka[slot] += dot(score_grad, qt, NN)
            part = dot(k, score_grad, TN)
            total = part if total is None else total + part
        dq[rows, :] = (total * SCALE).T.astype(BF16)
    dko[...] = dka[1:3].reshape(2 * TILE, HEAD)
    dvo[...] = dva[1:3].reshape(2 * TILE, HEAD)
    low[0] = dka[0].astype(BF16)
    low[1] = dva[0].astype(BF16)
    high[0] = dka[3].astype(BF16)
    high[1] = dva[3].astype(BF16)


def attend(meta, q, k, v, before, after, grads, o, norm, slabs, dq_full):
    per = slabs[0][0].shape[0] // HEAD
    heads = per * len(slabs)
    half = slabs[0][0].shape[1]
    own = pl.BlockSpec((2 * TILE, HEAD), lambda i, m: (0, m[HEADS_AT + i]))
    rim_k = pl.BlockSpec((1, TILE, HEAD), lambda i, m: (0, 0, m[HEADS_AT + i]))
    rim_v = pl.BlockSpec((1, TILE, HEAD), lambda i, m: (1, 0, m[HEADS_AT + i]))
    local = pl.BlockSpec((2 * TILE, HEAD), lambda i, m: (0, i))
    local_rim = pl.BlockSpec((2, TILE, HEAD), lambda i, m: (0, 0, i))
    near = pl.BlockSpec((2 * TILE, half), lambda i, m: (0, m[6]))
    away = pl.BlockSpec((2 * TILE, half), lambda i, m: (0, 1 - m[6]))
    slab = pl.BlockSpec((per * HEAD, half), lambda i, m: (0, 0))
    whole = pl.BlockSpec(norm.shape, lambda i, m: (0, 0))
    anywhere = pl.BlockSpec(memory_space=pl.ANY)
    wide = jax.ShapeDtypeStruct((2 * TILE, heads * HEAD), F32)
    rims = jax.ShapeDtypeStruct((2, TILE, heads * HEAD), BF16)
    flops = heads * (6 * 5 * 2 * TILE * TILE * HEAD * 3 + 2 * 2 * TILE * 2 * half * HEAD)
    flat = [w for pair in slabs for w in pair]
    return pl.pallas_call(
        functools.partial(attend_kernel, len(slabs)),
        grid_spec=pltpu.PrefetchScalarGridSpec(
            num_scalar_prefetch=1,
            grid=(heads,),
            in_specs=[own, rim_k, own, rim_k, rim_v, own, rim_v, near, away, own, whole]
            + [slab] * len(flat)
            + [anywhere],
            out_specs=[own, local, local, local_rim, local_rim],
            scratch_shapes=[
                pltpu.VMEM((4, TILE, HEAD), BF16),
                pltpu.VMEM((4, TILE, HEAD), BF16),
                pltpu.VMEM((4, TILE, HEAD), F32),
                pltpu.VMEM((4, TILE, HEAD), F32),
                pltpu.VMEM((per, 2 * TILE, HEAD), BF16),
            ],
        ),
        out_shape=[jax.ShapeDtypeStruct(q.shape, BF16), wide, wide, rims, rims],
        input_output_aliases={12 + len(flat): 0},
        compiler_params=pltpu.CompilerParams(vmem_limit_bytes=40 << 20),
        cost_estimate=pl.CostEstimate(
            flops=flops, bytes_accessed=heads * 3_000_000, transcendentals=heads * 6 * TILE * TILE
        ),
    )(meta, q, before, k, after, before, v, after, grads, grads, o, norm, *flat, dq_full)


def combine_kernel(meta, dko, dvo, below, above, dk_in, dv_in, dk, dv):
    dk[:TILE] = ((dko[:TILE] + below[0].astype(F32)) * SCALE).astype(BF16)
    dk[TILE:] = ((dko[TILE:] + above[0].astype(F32)) * SCALE).astype(BF16)
    dv[:TILE] = (dvo[:TILE] + below[1].astype(F32)).astype(BF16)
    dv[TILE:] = (dvo[TILE:] + above[1].astype(F32)).astype(BF16)


def combine(meta, dko, dvo, below, above, dk_full, dv_full):
    width = dko.shape[1]
    own = pl.BlockSpec((2 * TILE, HEAD), lambda i, m: (0, i))
    rim = pl.BlockSpec((2, TILE, HEAD), lambda i, m: (0, 0, i))
    placed = pl.BlockSpec((2 * TILE, HEAD), lambda i, m: (0, m[HEADS_AT + i]))
    anywhere = pl.BlockSpec(memory_space=pl.ANY)
    full = jax.ShapeDtypeStruct(dk_full.shape, BF16)
    return pl.pallas_call(
        combine_kernel,
        grid_spec=pltpu.PrefetchScalarGridSpec(
            num_scalar_prefetch=1,
            grid=(width // HEAD,),
            in_specs=[own, own, rim, rim, anywhere, anywhere],
            out_specs=[placed, placed],
        ),
        out_shape=[full, full],
        input_output_aliases={5: 0, 6: 1},
        compiler_params=pltpu.CompilerParams(vmem_limit_bytes=16 << 20),
        cost_estimate=pl.CostEstimate(
            flops=4_000_000, bytes_accessed=width * 20_000, transcendentals=0
        ),
    )(meta, dko, dvo, below, above, dk_full, dv_full)


def product_kernel(which, a, b, *refs):
    out, turned = refs[-2:]

    @pl.when(pl.program_id(1) == 0)
    def _():
        turned[...] = a[...].T

    made = dot(turned[...], b[...], NN)
    zs, xs, ds, rows, columns = out.shape
    for d in range(ds):
        for z in range(zs):
            for x in range(xs):
                at = (d * zs + z) * rows
                part = made[at : at + rows, x * columns : (x + 1) * columns]
                if len(refs) == 3:
                    part = part + refs[0][z, x, d].astype(F32)
                out[z, x, d] = part.astype(BF16)


def product(which, a, b, n_z, n_x, n_dp, *added):
    tokens, width = a.shape
    half = b.shape[1] // 2
    rows, columns = width // n_dp // n_z, half // n_x
    shape = (n_z, n_x, n_dp, rows, columns)
    block = pl.BlockSpec((n_z, 2, 2, rows, columns), lambda i, j, m: (0, j, i, 0, 0))
    steps = n_x // 2
    return pl.pallas_call(
        product_kernel,
        grid_spec=pltpu.PrefetchScalarGridSpec(
            num_scalar_prefetch=1,
            grid=(n_dp // 2, steps),
            in_specs=[
                pl.BlockSpec((tokens, 2 * n_z * rows), lambda i, j, m: (0, i)),
                pl.BlockSpec((tokens, 2 * columns), lambda i, j, m: (0, m[0] * steps + j)),
            ]
            + [block] * len(added),
            out_specs=block,
            scratch_shapes=[pltpu.VMEM((2 * n_z * rows, tokens), BF16)],
        ),
        out_shape=jax.ShapeDtypeStruct(shape, BF16),
        compiler_params=pltpu.CompilerParams(vmem_limit_bytes=40 << 20),
        cost_estimate=pl.CostEstimate(
            flops=2 * 2 * tokens * width * half, bytes_accessed=20_000_000, transcendentals=0
        ),
    )(which, a, b, *added)


def body(query, key_states, value_states, attn_out, log_norm, out_grad, out_weight, tile_lists):
    grad_rows = out_grad[0]
    out_rows = attn_out[0]
    q, k, v = query[0], key_states[0], value_states[0]
    norm = log_norm[0]
    tokens, width = q.shape
    model = grad_rows.shape[1]
    n_dp = lax.axis_size("dp")
    n_seq = lax.axis_size("seq")
    dp = lax.axis_index("dp")
    seq = lax.axis_index("seq")
    y = dp // 2
    core = seq % 2
    n_y = n_dp // 2
    n_x = 4
    n_z = n_seq // 2 // n_x

    def over_dp(value, target):
        return lax.ppermute(value, "dp", [(i, target(i)) for i in range(n_dp)])

    def over_seq(value, target):
        pairs = [(i, target(i)) for i in range(n_seq)]
        return lax.ppermute(value, "seq", [(i, j) for i, j in pairs if 0 <= j < n_seq])

    def swap(value):
        return over_seq(value, lambda i: i ^ 1)

    def up(value):
        return over_dp(value, lambda i: (i + 2) % n_dp)

    def down(value):
        return over_dp(value, lambda i: (i - 2) % n_dp)

    half = model // 2
    mine = lax.dynamic_slice_in_dim(out_weight, core * half, half, 1)
    other = over_dp(mine, lambda i: i ^ 1)
    before = over_seq(jnp.stack([k[tokens - TILE :], v[tokens - TILE :]]), lambda i: i + 1)
    after = over_seq(jnp.stack([k[:TILE], v[:TILE]]), lambda i: i - 1)
    low_first = dp % 2 == 0
    pair0 = jnp.concatenate(
        [jnp.where(low_first, mine, other), jnp.where(low_first, other, mine)], axis=0
    )
    from_up = up(pair0)
    from_down = down(pair0)
    far = up(from_up)
    order = [[(pair0, y)], [(from_up, y + n_y - 1), (from_down, y + 1)], [(far, y + 2)]]

    first_tile = seq * 2 - 1
    slots = (lax.dynamic_slice_in_dim(tile_lists[0], seq * 2, 2, 0) - first_tile).reshape(-1)

    sent = product((1 - core)[None], out_rows, grad_rows, n_z, n_x, n_dp)
    chip_sum = product(core[None], out_rows, grad_rows, n_z, n_x, n_dp, swap(sent))
    chips = [[2 * i + c for i in range(n_seq // 2)] for c in range(2)]
    piece = chip_sum.shape[-2:]
    spread = lax.all_to_all(
        chip_sum.reshape(n_seq // 2, n_dp, *piece), "seq", 0, 0, axis_index_groups=chips
    )
    clip_sum = spread.astype(F32).sum(0).astype(BF16)

    per = width // n_y // HEAD
    dq = jnp.zeros((tokens, width), BF16)
    dk = jnp.zeros((tokens, width), BF16)
    dv = jnp.zeros((tokens, width), BF16)
    pending = []
    for group in order:
        slabs = [(slab, swap(slab)) for slab, _ in group]
        heads = [(at % n_y) * per + jnp.arange(per, dtype=jnp.int32) for _, at in group]
        meta = jnp.concatenate([slots, core[None], *heads]).astype(jnp.int32)
        dq, dko, dvo, low, high = attend(
            meta, q, k, v, before, after, grad_rows, out_rows, norm, slabs, dq
        )
        below = over_seq(high, lambda i: i + 1)
        above = over_seq(low, lambda i: i - 1)
        pending.append((meta, dko, dvo, below, above))

    met = lax.all_to_all(clip_sum, "dp", 0, 0)
    total = met.astype(F32).sum(0).astype(BF16)
    ready = lax.all_to_all(jnp.broadcast_to(total, (n_seq, *piece)), "seq", 0, 0)
    weight_grad = (
        ready.astype(F32)
        .reshape(n_z, n_x, 2, *piece)
        .transpose(0, 3, 2, 1, 4)
        .reshape(width // n_dp, model)
    )

    for item in pending:
        dk, dv = combine(*item, dk, dv)
    return (dq[None], dk[None], dv[None], weight_grad)


def solution(mesh):
    placed = (
        P("dp", "seq", None),
        P("dp", "seq", None),
        P("dp", "seq", None),
        P("dp", "seq", None),
        P("dp", None, "seq"),
        P("dp", "seq", None),
        P("dp", None),
        P("dp", None, None),
    )
    return jax.shard_map(
        body,
        mesh=mesh,
        in_specs=placed,
        out_specs=(P("dp", "seq", None), P("dp", "seq", None), P("dp", "seq", None), P("dp", None)),
        check_vma=False,
    )
```

```python
import functools
import math

import jax
import jax.numpy as jnp
from jax import lax
from jax.experimental import pallas as pl
from jax.experimental.pallas import tpu as pltpu
from jax.sharding import PartitionSpec as P

TILE = 384
HEAD = 128
LOG2E = math.log2(math.e)
SCALE = 1.0 / math.sqrt(HEAD)
F32 = jnp.float32
BF16 = jnp.bfloat16
NT = (((1,), (1,)), ((), ()))
NN = (((1,), (0,)), ((), ()))
TN = (((0,), (0,)), ((), ()))


def dot(a, b, dims):
    return lax.dot_general(a, b, dims, preferred_element_type=F32)


HEADS_AT = 7
VMEM = 62 << 20


def attend_kernel(slabs, *refs):
    meta, q, kb, ko, ka, vb, vo, va, near, away, o, norm = refs[:12]
    weights_in = refs[12 : 12 + 2 * slabs]
    dq, dko, dvo, low, high, kw, vw, dka, dva, gs = refs[-10:]
    step = pl.program_id(0)
    head = meta[HEADS_AT + step]
    per = gs.shape[0]
    for n in range(slabs):

        @pl.when(step == n * per)
        def _(n=n):
            made = dot(near[...], weights_in[2 * n][...], NT)
            made += dot(away[...], weights_in[2 * n + 1][...], NT)
            for m in range(per):
                gs[m] = made[:, m * HEAD : (m + 1) * HEAD].astype(BF16)

    g = gs.at[lax.rem(step, per)]
    kw[0] = kb[0]
    kw[1] = ko[:TILE]
    kw[2] = ko[TILE:]
    kw[3] = ka[0]
    vw[0] = vb[0]
    vw[1] = vo[:TILE]
    vw[2] = vo[TILE:]
    vw[3] = va[0]
    dka[...] = jnp.zeros_like(dka)
    dva[...] = jnp.zeros_like(dva)
    ones = jnp.ones((16, HEAD), BF16)
    for t in range(2):
        rows = slice(t * TILE, (t + 1) * TILE)
        qt = q[rows, :]
        gt = g[rows, :]
        prod = gt.astype(F32) * o[rows, :].astype(F32)
        coarse = prod.astype(BF16)
        fine = (prod - coarse.astype(F32)).astype(BF16)
        delta = (dot(ones, coarse, NT) + dot(ones, fine, NT))[0:1]
        shift = norm[pl.ds(head, 1), rows] * LOG2E
        total = None
        for j in range(3):
            slot = meta[t * 3 + j]
            k = kw[slot]
            weights = jnp.exp2(dot(k, qt, NT) * (SCALE * LOG2E) - shift)
            score_grad = (weights * (dot(vw[slot], gt, NT) - delta)).astype(BF16)
            dva[slot] += dot(weights.astype(BF16), gt, NN)
            dka[slot] += dot(score_grad, qt, NN)
            part = dot(k, score_grad, TN)
            total = part if total is None else total + part
        dq[rows, :] = (total * SCALE).T.astype(BF16)
    dko[...] = dka[1:3].reshape(2 * TILE, HEAD)
    dvo[...] = dva[1:3].reshape(2 * TILE, HEAD)
    low[0] = dka[0].astype(BF16)
    low[1] = dva[0].astype(BF16)
    high[0] = dka[3].astype(BF16)
    high[1] = dva[3].astype(BF16)


def attend(meta, q, k, v, before, after, grads, o, norm, slabs, dq_full):
    per = slabs[0][0].shape[0] // HEAD
    heads = per * len(slabs)
    half = slabs[0][0].shape[1]
    own = pl.BlockSpec((2 * TILE, HEAD), lambda i, m: (0, m[HEADS_AT + i]))
    rim_k = pl.BlockSpec((1, TILE, HEAD), lambda i, m: (0, 0, m[HEADS_AT + i]))
    rim_v = pl.BlockSpec((1, TILE, HEAD), lambda i, m: (1, 0, m[HEADS_AT + i]))
    local = pl.BlockSpec((2 * TILE, HEAD), lambda i, m: (0, i))
    local_rim = pl.BlockSpec((2, TILE, HEAD), lambda i, m: (0, 0, i))
    near = pl.BlockSpec((2 * TILE, half), lambda i, m: (0, m[6]))
    away = pl.BlockSpec((2 * TILE, half), lambda i, m: (0, 1 - m[6]))
    slab = pl.BlockSpec((per * HEAD, half), lambda i, m: (0, 0))
    whole = pl.BlockSpec(norm.shape, lambda i, m: (0, 0))
    anywhere = pl.BlockSpec(memory_space=pl.ANY)
    wide = jax.ShapeDtypeStruct((2 * TILE, heads * HEAD), F32)
    rims = jax.ShapeDtypeStruct((2, TILE, heads * HEAD), BF16)
    flops = heads * (6 * 5 * 2 * TILE * TILE * HEAD + 2 * 2 * TILE * 2 * half * HEAD)
    flat = [w for pair in slabs for w in pair]
    full = [] if dq_full is None else [dq_full]
    return pl.pallas_call(
        functools.partial(attend_kernel, len(slabs)),
        grid_spec=pltpu.PrefetchScalarGridSpec(
            num_scalar_prefetch=1,
            grid=(heads,),
            in_specs=[own, rim_k, own, rim_k, rim_v, own, rim_v, near, away, own, whole]
            + [slab] * len(flat)
            + [anywhere] * len(full),
            out_specs=[own, local, local, local_rim, local_rim],
            scratch_shapes=[
                pltpu.VMEM((4, TILE, HEAD), BF16),
                pltpu.VMEM((4, TILE, HEAD), BF16),
                pltpu.VMEM((4, TILE, HEAD), F32),
                pltpu.VMEM((4, TILE, HEAD), F32),
                pltpu.VMEM((per, 2 * TILE, HEAD), BF16),
            ],
        ),
        out_shape=[jax.ShapeDtypeStruct(q.shape, BF16), wide, wide, rims, rims],
        input_output_aliases={12 + len(flat): 0} if full else {},
        compiler_params=pltpu.CompilerParams(vmem_limit_bytes=VMEM),
        cost_estimate=pl.CostEstimate(
            flops=flops, bytes_accessed=heads * 2_000_000, transcendentals=heads * 6 * TILE * TILE
        ),
    )(meta, q, before, k, after, before, v, after, grads, grads, o, norm, *flat, *full)


def combine_kernel(edges, meta, *refs):
    dk, dv = refs[-2:]
    step = pl.program_id(0)
    for n, (start, stop) in enumerate(edges):
        dko, dvo, below, above = refs[4 * n : 4 * n + 4]

        @pl.when((step >= start) & (step < stop))
        def _(dko=dko, dvo=dvo, below=below, above=above):
            dk[:TILE] = ((dko[:TILE] + below[0].astype(F32)) * SCALE).astype(BF16)
            dk[TILE:] = ((dko[TILE:] + above[0].astype(F32)) * SCALE).astype(BF16)
            dv[:TILE] = (dvo[:TILE] + below[1].astype(F32)).astype(BF16)
            dv[TILE:] = (dvo[TILE:] + above[1].astype(F32)).astype(BF16)


def combine(blocks, groups, *filled):
    edges, in_specs, flat, start = [], [], [], 0
    wide = min(group[0].shape[1] for group in groups)
    width = blocks[1] * wide
    anywhere = pl.BlockSpec(memory_space=pl.ANY)
    for group in groups:
        count = group[0].shape[1] // wide

        def at(i, start=start, count=count):
            return jnp.clip(i - start, 0, count - 1)

        own = pl.BlockSpec((2 * TILE, wide), lambda i, m, at=at: (0, at(i)))
        rim = pl.BlockSpec((2, TILE, wide), lambda i, m, at=at: (0, 0, at(i)))
        in_specs += [own, own, rim, rim]
        flat += group
        edges.append((start, start + count))
        start += count
    placed = pl.BlockSpec((2 * TILE, wide), lambda i, m: (0, m[i]))
    return pl.pallas_call(
        functools.partial(combine_kernel, edges),
        grid_spec=pltpu.PrefetchScalarGridSpec(
            num_scalar_prefetch=1,
            grid=(start,),
            in_specs=in_specs + [anywhere] * len(filled),
            out_specs=[placed, placed],
        ),
        out_shape=[jax.ShapeDtypeStruct((2 * TILE, width), BF16)] * 2,
        input_output_aliases={1 + len(flat) + n: n for n in range(len(filled))},
        compiler_params=pltpu.CompilerParams(vmem_limit_bytes=VMEM),
        cost_estimate=pl.CostEstimate(
            flops=4_000_000, bytes_accessed=20_000_000, transcendentals=0
        ),
    )(blocks[0], *flat, *filled)


def product_kernel(which, a, b, *refs):
    out = refs[-1]
    added = refs[:-1]
    zs, xs, ds, rows, columns = out.shape
    turned = a[...].T
    for half in range(xs // 2):
        wide = 2 * columns
        made = dot(turned, b[:, half * wide : (half + 1) * wide], NN)
        for d in range(ds):
            for z in range(zs):
                for n in range(2):
                    at = (d * zs + z) * rows
                    part = made[at : at + rows, n * columns : (n + 1) * columns]
                    if added:
                        part = part + added[half][z, n, d].astype(F32)
                    out[z, 2 * half + n, d] = part.astype(BF16)


def product(which, a, b, n_z, n_x, n_dp, parts, *added):
    tokens, width = a.shape
    wide = b.shape[1] // 2 // parts
    rows, columns = width // n_dp // n_z, b.shape[1] // 2 // n_x
    shape = (n_z, n_x // parts, n_dp, rows, columns)
    block = pl.BlockSpec((n_z, n_x // parts, 2, rows, columns), lambda i, m: (0, 0, i, 0, 0))
    piece = pl.BlockSpec((n_z, 2, 2, rows, columns), lambda i, m: (0, 0, i, 0, 0))
    return pl.pallas_call(
        product_kernel,
        grid_spec=pltpu.PrefetchScalarGridSpec(
            num_scalar_prefetch=1,
            grid=(n_dp // 2,),
            in_specs=[
                pl.BlockSpec((tokens, 2 * n_z * rows), lambda i, m: (0, i)),
                pl.BlockSpec((tokens, wide), lambda i, m: (0, m[0])),
            ]
            + [piece] * len(added),
            out_specs=block,
        ),
        out_shape=jax.ShapeDtypeStruct(shape, BF16),
        compiler_params=pltpu.CompilerParams(vmem_limit_bytes=VMEM),
        cost_estimate=pl.CostEstimate(
            flops=tokens * width * wide // 16, bytes_accessed=400_000, transcendentals=0
        ),
    )(which, a, b, *added)


def lay_kernel(pieces, out):
    n_x = pieces.shape[0] // 2
    columns = pieces.shape[2]
    for x in range(n_x):
        for c in range(2):
            at = (c * n_x + x) * columns
            out[:, at : at + columns] = pieces[2 * x + c].astype(F32)


def lay_out(pieces, n_z):
    count, rows, columns = pieces.shape
    wide = count // n_z * columns
    return pl.pallas_call(
        lay_kernel,
        grid=(n_z,),
        in_specs=[pl.BlockSpec((count // n_z, rows, columns), lambda i: (i, 0, 0))],
        out_specs=pl.BlockSpec((rows, wide), lambda i: (i, 0)),
        out_shape=jax.ShapeDtypeStruct((n_z * rows, wide), F32),
        compiler_params=pltpu.CompilerParams(vmem_limit_bytes=VMEM),
    )(pieces)


def pack_kernel(kf, kl, vf, vl, last, first):
    last[0] = kl[...]
    last[1] = vl[...]
    first[0] = kf[...]
    first[1] = vf[...]


def pack(k, v):
    steps = 3
    columns = k.shape[1] // steps
    end = k.shape[0] // TILE - 1
    head = pl.BlockSpec((TILE, columns), lambda i: (0, i))
    tail = pl.BlockSpec((TILE, columns), lambda i: (end, i))
    rim = pl.BlockSpec((2, TILE, columns), lambda i: (0, 0, i))
    shape = jax.ShapeDtypeStruct((2, TILE, k.shape[1]), BF16)
    return pl.pallas_call(
        pack_kernel,
        grid=(steps,),
        in_specs=[head, tail, head, tail],
        out_specs=[rim, rim],
        out_shape=[shape, shape],
        compiler_params=pltpu.CompilerParams(vmem_limit_bytes=VMEM),
    )(k, k, v, v)


def body(query, key_states, value_states, attn_out, log_norm, out_grad, out_weight, tile_lists):
    grad_rows = out_grad[0]
    out_rows = attn_out[0]
    q, k, v = query[0], key_states[0], value_states[0]
    norm = log_norm[0]
    tokens, width = q.shape
    model = grad_rows.shape[1]
    n_dp = lax.axis_size("dp")
    n_seq = lax.axis_size("seq")
    dp = lax.axis_index("dp")
    seq = lax.axis_index("seq")
    y = dp // 2
    core = seq % 2
    n_y = n_dp // 2
    n_x = 4
    n_z = n_seq // 2 // n_x

    def over_dp(value, target):
        return lax.ppermute(value, "dp", [(i, target(i)) for i in range(n_dp)])

    def over_seq(value, target):
        pairs = [(i, target(i)) for i in range(n_seq)]
        return lax.ppermute(value, "seq", [(i, j) for i, j in pairs if 0 <= j < n_seq])

    def swap(value):
        return over_seq(value, lambda i: i ^ 1)

    def up(value):
        return over_dp(value, lambda i: (i + 2) % n_dp)

    def down(value):
        return over_dp(value, lambda i: (i - 2) % n_dp)

    half = model // 2
    mine = lax.dynamic_slice_in_dim(out_weight, core * half, half, 1)
    last, first = pack(k, v)
    mine, last, first, left = lax.optimization_barrier((mine, last, first, out_rows))
    before = over_seq(last, lambda i: i + 1)
    after = over_seq(first, lambda i: i - 1)
    other = over_dp(mine, lambda i: i ^ 1)

    first_tile = seq * 2 - 1
    slots = (lax.dynamic_slice_in_dim(tile_lists[0], seq * 2, 2, 0) - first_tile).reshape(-1)

    send = 2 * (1 - core)
    sent0 = product(send[None], left, grad_rows, n_z, n_x, n_dp, 2)
    left, other = lax.optimization_barrier((left, other))
    sent1 = product((send + 1)[None], left, grad_rows, n_z, n_x, n_dp, 2)
    low_first = dp % 2 == 0
    pair0 = jnp.concatenate(
        [jnp.where(low_first, mine, other), jnp.where(low_first, other, mine)], axis=0
    )
    from_up = up(pair0)
    from_down = down(pair0)
    across0 = swap(pair0)
    met0, met1, before, after = lax.optimization_barrier((swap(sent0), swap(sent1), before, after))
    chip_sum = product(core[None], out_rows, grad_rows, n_z, n_x, n_dp, 1, met0, met1)
    chip_sum, across0 = lax.optimization_barrier((chip_sum, across0))
    chips = [[2 * i + c for i in range(n_seq // 2)] for c in range(2)]
    piece = chip_sum.shape[-2:]
    spread = lax.all_to_all(
        chip_sum.reshape(n_seq // 2, n_dp, *piece), "seq", 0, 0, axis_index_groups=chips
    )

    per = width // n_y // HEAD
    pending = []

    def attend_group(ats, slabs, dq):
        heads = [(at % n_y) * per + jnp.arange(per, dtype=jnp.int32) for at in ats]
        heads = jnp.concatenate(heads).astype(jnp.int32)
        meta = jnp.concatenate([slots, core[None], heads]).astype(jnp.int32)
        dq, dko, dvo, low, high = attend(
            meta, q, k, v, before, after, grad_rows, out_rows, norm, slabs, dq
        )
        below = over_seq(high, lambda i: i + 1)
        above = over_seq(low, lambda i: i - 1)
        pending.append([dko, dvo, below, above])
        return dq

    dq = attend_group([y], [(pair0, across0)], None)
    from_up, from_down, dq = lax.optimization_barrier((from_up, from_down, dq))
    far = up(from_up)
    dq = attend_group(
        [y + n_y - 1, y + 1], [(from_up, swap(from_up)), (from_down, swap(from_down))], dq
    )
    spread, far, dq = lax.optimization_barrier((spread, far, dq))
    clip_sum = spread.astype(F32).sum(0).astype(BF16)
    dq = attend_group([y + 2], [(far, swap(far))], dq)

    met = lax.all_to_all(clip_sum, "dp", 0, 0)
    met, dq, *rims = lax.optimization_barrier((met, dq, *pending[0][2:], *pending[1][2:]))
    pending[0][2:], pending[1][2:] = rims[:2], rims[2:]
    total = met.astype(F32).sum(0).astype(BF16)
    ready = lax.all_to_all(jnp.broadcast_to(total, (n_seq, *piece)), "seq", 0, 0)
    weight_grad = lay_out(ready, n_z)

    blocks = jnp.stack([y, (y + n_y - 1) % n_y, (y + 1) % n_y, (y + 2) % n_y]).astype(jnp.int32)
    filled = combine((blocks[:3], n_y), pending[:2])
    dk, dv = combine((blocks[3:], n_y), pending[2:], *filled)
    return (dq[None], dk[None], dv[None], weight_grad)


def solution(mesh):
    placed = (
        P("dp", "seq", None),
        P("dp", "seq", None),
        P("dp", "seq", None),
        P("dp", "seq", None),
        P("dp", None, "seq"),
        P("dp", "seq", None),
        P("dp", None),
        P("dp", None, None),
    )
    return jax.shard_map(
        body,
        mesh=mesh,
        in_specs=placed,
        out_specs=(P("dp", "seq", None), P("dp", "seq", None), P("dp", "seq", None), P("dp", None)),
        check_vma=False,
    )
```

```python
import functools
import math

import jax
import jax.numpy as jnp
from jax import lax
from jax.experimental import pallas as pl
from jax.experimental.pallas import tpu as pltpu
from jax.sharding import PartitionSpec as P

TILE = 384
HEAD = 128
LOG2E = math.log2(math.e)
SCALE = 1.0 / math.sqrt(HEAD)
F32 = jnp.float32
BF16 = jnp.bfloat16
NT = (((1,), (1,)), ((), ()))
NN = (((1,), (0,)), ((), ()))
TN = (((0,), (0,)), ((), ()))


def dot(a, b, dims):
    return lax.dot_general(a, b, dims, preferred_element_type=F32)


HEADS_AT = 7
VMEM = 62 << 20


def attend_kernel(slabs, *refs):
    meta, q, kb, ko, ka, vb, vo, va, o, norm = refs[:10]
    step = pl.program_id(0)
    head = meta[HEADS_AT + step]
    if slabs:
        near, away = refs[10:12]
        weights_in = refs[12 : 12 + 2 * slabs]
        dq, dko, dvo, low, high, kw, vw, dka, dva, gs = refs[-10:]
        per = gs.shape[0]
        for n in range(slabs):

            @pl.when(step == n * per)
            def _(n=n):
                made = dot(near[...], weights_in[2 * n][...], NT)
                made += dot(away[...], weights_in[2 * n + 1][...], NT)
                for m in range(per):
                    gs[m] = made[:, m * HEAD : (m + 1) * HEAD].astype(BF16)

        g = gs.at[lax.rem(step, per)]
    else:
        g = refs[10]
        dq, dko, dvo, low, high, kw, vw, dka, dva = refs[-9:]
    kw[0] = kb[0]
    kw[1] = ko[:TILE]
    kw[2] = ko[TILE:]
    kw[3] = ka[0]
    vw[0] = vb[0]
    vw[1] = vo[:TILE]
    vw[2] = vo[TILE:]
    vw[3] = va[0]
    dka[...] = jnp.zeros_like(dka)
    dva[...] = jnp.zeros_like(dva)
    ones = jnp.ones((16, HEAD), BF16)
    for t in range(2):
        rows = slice(t * TILE, (t + 1) * TILE)
        qt = q[rows, :]
        gt = g[rows, :]
        prod = gt.astype(F32) * o[rows, :].astype(F32)
        coarse = prod.astype(BF16)
        fine = (prod - coarse.astype(F32)).astype(BF16)
        delta = (dot(ones, coarse, NT) + dot(ones, fine, NT))[0:1]
        shift = norm[pl.ds(head, 1), rows] * LOG2E
        total = None
        for j in range(3):
            slot = meta[t * 3 + j]
            k = kw[slot]
            weights = jnp.exp2(dot(k, qt, NT) * (SCALE * LOG2E) - shift)
            score_grad = (weights * (dot(vw[slot], gt, NT) - delta)).astype(BF16)
            dva[slot] += dot(weights.astype(BF16), gt, NN)
            dka[slot] += dot(score_grad, qt, NN)
            part = dot(k, score_grad, TN)
            total = part if total is None else total + part
        dq[rows, :] = (total * SCALE).T.astype(BF16)
    dko[...] = dka[1:3].reshape(2 * TILE, HEAD)
    dvo[...] = dva[1:3].reshape(2 * TILE, HEAD)
    low[0] = dka[0].astype(BF16)
    low[1] = dva[0].astype(BF16)
    high[0] = dka[3].astype(BF16)
    high[1] = dva[3].astype(BF16)


def attend(meta, q, k, v, before, after, o, norm, g, slabs, grads, width, start, filled):
    heads = meta.shape[0] - HEADS_AT
    own = pl.BlockSpec((2 * TILE, HEAD), lambda i, m: (0, m[HEADS_AT + i]))
    rim_k = pl.BlockSpec((1, TILE, HEAD), lambda i, m: (0, 0, m[HEADS_AT + i]))
    rim_v = pl.BlockSpec((1, TILE, HEAD), lambda i, m: (1, 0, m[HEADS_AT + i]))
    local = pl.BlockSpec((2 * TILE, HEAD), lambda i, m: (0, i + start))
    local_rim = pl.BlockSpec((2, TILE, HEAD), lambda i, m: (0, 0, i + start))
    whole = pl.BlockSpec(norm.shape, lambda i, m: (0, 0))
    anywhere = pl.BlockSpec(memory_space=pl.ANY)
    wide = jax.ShapeDtypeStruct((2 * TILE, width), F32)
    rims = jax.ShapeDtypeStruct((2, TILE, width), BF16)
    in_specs = [own, rim_k, own, rim_k, rim_v, own, rim_v, own, whole]
    operands = [q, before, k, after, before, v, after, o, norm]
    scratch = [
        pltpu.VMEM((4, TILE, HEAD), BF16),
        pltpu.VMEM((4, TILE, HEAD), BF16),
        pltpu.VMEM((4, TILE, HEAD), F32),
        pltpu.VMEM((4, TILE, HEAD), F32),
    ]
    flops = heads * 6 * 5 * 2 * TILE * TILE * HEAD
    if slabs:
        rows, half = slabs[0][0].shape
        in_specs += [
            pl.BlockSpec((2 * TILE, half), lambda i, m: (0, m[6])),
            pl.BlockSpec((2 * TILE, half), lambda i, m: (0, 1 - m[6])),
        ]
        in_specs += [pl.BlockSpec((rows, half), lambda i, m: (0, 0))] * (2 * len(slabs))
        operands += [grads, grads, *(w for pair in slabs for w in pair)]
        scratch.append(pltpu.VMEM((rows // HEAD, 2 * TILE, HEAD), BF16))
        flops += heads * 2 * 2 * TILE * 2 * half * HEAD
    else:
        in_specs.append(pl.BlockSpec((2 * TILE, HEAD), lambda i, m: (0, i)))
        operands.append(g)
    return pl.pallas_call(
        functools.partial(attend_kernel, len(slabs)),
        grid_spec=pltpu.PrefetchScalarGridSpec(
            num_scalar_prefetch=1,
            grid=(heads,),
            in_specs=in_specs + [anywhere] * len(filled),
            out_specs=[own, local, local, local_rim, local_rim],
            scratch_shapes=scratch,
        ),
        out_shape=[jax.ShapeDtypeStruct(q.shape, BF16), wide, wide, rims, rims],
        input_output_aliases={1 + len(operands) + n: n for n in range(len(filled))},
        compiler_params=pltpu.CompilerParams(vmem_limit_bytes=VMEM),
        cost_estimate=pl.CostEstimate(
            flops=flops, bytes_accessed=heads * 2_000_000, transcendentals=heads * 6 * TILE * TILE
        ),
    )(meta, *operands, *filled)


def combine_kernel(edges, meta, *refs):
    dk, dv = refs[-2:]
    step = pl.program_id(0)
    for n, (start, stop) in enumerate(edges):
        dko, dvo, below, above = refs[4 * n : 4 * n + 4]

        @pl.when((step >= start) & (step < stop))
        def _(dko=dko, dvo=dvo, below=below, above=above):
            dk[:TILE] = ((dko[:TILE] + below[0].astype(F32)) * SCALE).astype(BF16)
            dk[TILE:] = ((dko[TILE:] + above[0].astype(F32)) * SCALE).astype(BF16)
            dv[:TILE] = (dvo[:TILE] + below[1].astype(F32)).astype(BF16)
            dv[TILE:] = (dvo[TILE:] + above[1].astype(F32)).astype(BF16)


def combine(blocks, groups, *filled):
    edges, in_specs, flat, start = [], [], [], 0
    wide = blocks[2]
    width = blocks[1] * wide
    anywhere = pl.BlockSpec(memory_space=pl.ANY)
    for group in groups:
        count = group[0].shape[1] // wide

        def at(i, start=start, count=count):
            return jnp.clip(i - start, 0, count - 1)

        own = pl.BlockSpec((2 * TILE, wide), lambda i, m, at=at: (0, at(i)))
        rim = pl.BlockSpec((2, TILE, wide), lambda i, m, at=at: (0, 0, at(i)))
        in_specs += [own, own, rim, rim]
        flat += group
        edges.append((start, start + count))
        start += count
    placed = pl.BlockSpec((2 * TILE, wide), lambda i, m: (0, m[i]))
    return pl.pallas_call(
        functools.partial(combine_kernel, edges),
        grid_spec=pltpu.PrefetchScalarGridSpec(
            num_scalar_prefetch=1,
            grid=(start,),
            in_specs=in_specs + [anywhere] * len(filled),
            out_specs=[placed, placed],
        ),
        out_shape=[jax.ShapeDtypeStruct((2 * TILE, width), BF16)] * 2,
        input_output_aliases={1 + len(flat) + n: n for n in range(len(filled))},
        compiler_params=pltpu.CompilerParams(vmem_limit_bytes=VMEM),
        cost_estimate=pl.CostEstimate(
            flops=4_000_000, bytes_accessed=20_000_000, transcendentals=0
        ),
    )(blocks[0], *flat, *filled)


def product_kernel(which, a, b, *refs):
    out = refs[-1]
    added = refs[:-1]
    zs, xs, ds, rows, columns = out.shape
    turned = a[...].T
    for half in range(xs // 2):
        wide = 2 * columns
        made = dot(turned, b[:, half * wide : (half + 1) * wide], NN)
        for d in range(ds):
            for z in range(zs):
                for n in range(2):
                    at = (d * zs + z) * rows
                    part = made[at : at + rows, n * columns : (n + 1) * columns]
                    if added:
                        part = part + added[half][z, n, d].astype(F32)
                    out[z, 2 * half + n, d] = part.astype(BF16)


def product(which, a, b, n_z, n_x, n_dp, parts, *added):
    tokens, width = a.shape
    wide = b.shape[1] // 2 // parts
    rows, columns = width // n_dp // n_z, b.shape[1] // 2 // n_x
    shape = (n_z, n_x // parts, n_dp, rows, columns)
    block = pl.BlockSpec((n_z, n_x // parts, 2, rows, columns), lambda i, m: (0, 0, i, 0, 0))
    piece = pl.BlockSpec((n_z, 2, 2, rows, columns), lambda i, m: (0, 0, i, 0, 0))
    return pl.pallas_call(
        product_kernel,
        grid_spec=pltpu.PrefetchScalarGridSpec(
            num_scalar_prefetch=1,
            grid=(n_dp // 2,),
            in_specs=[
                pl.BlockSpec((tokens, 2 * n_z * rows), lambda i, m: (0, i)),
                pl.BlockSpec((tokens, wide), lambda i, m: (0, m[0])),
            ]
            + [piece] * len(added),
            out_specs=block,
        ),
        out_shape=jax.ShapeDtypeStruct(shape, BF16),
        compiler_params=pltpu.CompilerParams(vmem_limit_bytes=VMEM),
        cost_estimate=pl.CostEstimate(
            flops=tokens * width * wide // 16, bytes_accessed=400_000, transcendentals=0
        ),
    )(which, a, b, *added)


def lay_kernel(pieces, out):
    n_x = pieces.shape[0] // 2
    columns = pieces.shape[2]
    for x in range(n_x):
        for c in range(2):
            at = (c * n_x + x) * columns
            out[:, at : at + columns] = pieces[2 * x + c].astype(F32)


def lay_out(pieces, n_z):
    count, rows, columns = pieces.shape
    wide = count // n_z * columns
    return pl.pallas_call(
        lay_kernel,
        grid=(n_z,),
        in_specs=[pl.BlockSpec((count // n_z, rows, columns), lambda i: (i, 0, 0))],
        out_specs=pl.BlockSpec((rows, wide), lambda i: (i, 0)),
        out_shape=jax.ShapeDtypeStruct((n_z * rows, wide), F32),
        compiler_params=pltpu.CompilerParams(vmem_limit_bytes=VMEM),
    )(pieces)


def pack_kernel(kf, kl, vf, vl, last, first):
    last[0] = kl[...]
    last[1] = vl[...]
    first[0] = kf[...]
    first[1] = vf[...]


def pack(k, v):
    steps = 3
    columns = k.shape[1] // steps
    end = k.shape[0] // TILE - 1
    head = pl.BlockSpec((TILE, columns), lambda i: (0, i))
    tail = pl.BlockSpec((TILE, columns), lambda i: (end, i))
    rim = pl.BlockSpec((2, TILE, columns), lambda i: (0, 0, i))
    shape = jax.ShapeDtypeStruct((2, TILE, k.shape[1]), BF16)
    return pl.pallas_call(
        pack_kernel,
        grid=(steps,),
        in_specs=[head, tail, head, tail],
        out_specs=[rim, rim],
        out_shape=[shape, shape],
        compiler_params=pltpu.CompilerParams(vmem_limit_bytes=VMEM),
    )(k, k, v, v)


def body(query, key_states, value_states, attn_out, log_norm, out_grad, out_weight, tile_lists):
    grad_rows = out_grad[0]
    out_rows = attn_out[0]
    q, k, v = query[0], key_states[0], value_states[0]
    norm = log_norm[0]
    tokens, width = q.shape
    model = grad_rows.shape[1]
    n_dp = lax.axis_size("dp")
    n_seq = lax.axis_size("seq")
    dp = lax.axis_index("dp")
    seq = lax.axis_index("seq")
    y = dp // 2
    core = seq % 2
    n_y = n_dp // 2
    n_x = 4
    n_z = n_seq // 2 // n_x

    def over_dp(value, target):
        return lax.ppermute(value, "dp", [(i, target(i)) for i in range(n_dp)])

    def over_seq(value, target):
        pairs = [(i, target(i)) for i in range(n_seq)]
        return lax.ppermute(value, "seq", [(i, j) for i, j in pairs if 0 <= j < n_seq])

    def swap(value):
        return over_seq(value, lambda i: i ^ 1)

    def up(value):
        return over_dp(value, lambda i: (i + 2) % n_dp)

    def down(value):
        return over_dp(value, lambda i: (i - 2) % n_dp)

    half = model // 2
    mine = lax.dynamic_slice_in_dim(out_weight, core * half, half, 1)
    last, first = pack(k, v)
    mine, last, first, left = lax.optimization_barrier((mine, last, first, out_rows))
    before = over_seq(last, lambda i: i + 1)
    after = over_seq(first, lambda i: i - 1)
    other = over_dp(mine, lambda i: i ^ 1)

    first_tile = seq * 2 - 1
    slots = (lax.dynamic_slice_in_dim(tile_lists[0], seq * 2, 2, 0) - first_tile).reshape(-1)

    send = 2 * (1 - core)
    sent0 = product(send[None], left, grad_rows, n_z, n_x, n_dp, 2)
    left, other = lax.optimization_barrier((left, other))
    sent1 = product((send + 1)[None], left, grad_rows, n_z, n_x, n_dp, 2)
    low_first = dp % 2 == 0
    pair0 = jnp.concatenate(
        [jnp.where(low_first, mine, other), jnp.where(low_first, other, mine)], axis=0
    )
    from_up = up(pair0)
    from_down = down(pair0)
    across0 = swap(pair0)
    rows_here = jnp.concatenate(
        [jnp.where(core == 0, pair0, across0), jnp.where(core == 0, across0, pair0)], axis=1
    )
    g0 = dot(grad_rows, rows_here, NT).astype(BF16)
    met0, met1, before, after, g0 = lax.optimization_barrier(
        (swap(sent0), swap(sent1), before, after, g0)
    )
    chip_sum = product(core[None], out_rows, grad_rows, n_z, n_x, n_dp, 1, met0, met1)
    chip_sum, g0, from_up, from_down = lax.optimization_barrier((chip_sum, g0, from_up, from_down))
    chips = [[2 * i + c for i in range(n_seq // 2)] for c in range(2)]
    piece = chip_sum.shape[-2:]
    spread = lax.all_to_all(
        chip_sum.reshape(n_seq // 2, n_dp, *piece), "seq", 0, 0, axis_index_groups=chips
    )

    per = width // n_y // HEAD

    def attend_group(ats, g, slabs, width, start, filled):
        heads = [(at % n_y) * per + jnp.arange(per, dtype=jnp.int32) for at in ats]
        meta = jnp.concatenate([slots, core[None], *heads]).astype(jnp.int32)
        return attend(
            meta, q, k, v, before, after, out_rows, norm, g, slabs, grad_rows, width, start, filled
        )

    def rims_of(low, high):
        return [over_seq(high, lambda i: i + 1), over_seq(low, lambda i: i - 1)]

    three = width // n_y
    far = up(from_up)
    across_up, across_down = swap(from_up), swap(from_down)
    begun = attend_group([y], g0, [], 3 * three, 0, [])
    most = attend_group(
        [y + n_y - 1, y + 1],
        None,
        [(from_up, across_up), (from_down, across_down)],
        3 * three,
        per,
        begun,
    )
    dq, dko, dvo, low, high = most
    spread, far, dq = lax.optimization_barrier((spread, far, dq))
    rims = rims_of(low, high)
    clip_sum = spread.astype(F32).sum(0).astype(BF16)
    dq, *rest = attend_group([y + 2], None, [(far, swap(far))], three, 0, [dq])
    pending = [[dko, dvo, *rims], [*rest[:2], *rims_of(*rest[2:])]]

    met = lax.all_to_all(clip_sum, "dp", 0, 0)
    met, dq, *rims = lax.optimization_barrier((met, dq, *pending[0][2:]))
    pending[0][2:] = rims
    total = met.astype(F32).sum(0).astype(BF16)
    ready = lax.all_to_all(jnp.broadcast_to(total, (n_seq, *piece)), "seq", 0, 0)
    weight_grad = lay_out(ready, n_z)

    blocks = jnp.stack([y, (y + n_y - 1) % n_y, (y + 1) % n_y, (y + 2) % n_y]).astype(jnp.int32)
    filled = combine((blocks[:3], n_y, three), pending[:1])
    dk, dv = combine((blocks[3:], n_y, three), pending[1:], *filled)
    return (dq[None], dk[None], dv[None], weight_grad)


def solution(mesh):
    placed = (
        P("dp", "seq", None),
        P("dp", "seq", None),
        P("dp", "seq", None),
        P("dp", "seq", None),
        P("dp", None, "seq"),
        P("dp", "seq", None),
        P("dp", None),
        P("dp", None, None),
    )
    return jax.shard_map(
        body,
        mesh=mesh,
        in_specs=placed,
        out_specs=(P("dp", "seq", None), P("dp", "seq", None), P("dp", "seq", None), P("dp", None)),
        check_vma=False,
    )
```

```python
import functools
import math

import jax
import jax.numpy as jnp
from jax import lax
from jax.experimental import pallas as pl
from jax.experimental.pallas import tpu as pltpu
from jax.sharding import PartitionSpec as P

TILE = 384
HEAD = 128
LOG2E = math.log2(math.e)
SCALE = 1.0 / math.sqrt(HEAD)
F32 = jnp.float32
BF16 = jnp.bfloat16
NT = (((1,), (1,)), ((), ()))
NN = (((1,), (0,)), ((), ()))
TN = (((0,), (0,)), ((), ()))


def dot(a, b, dims):
    return lax.dot_general(a, b, dims, preferred_element_type=F32)


HEADS_AT = 7
VMEM = 62 << 20


def attend_kernel(slabs, *refs):
    meta, q, kb, ko, ka, vb, vo, va, o, norm = refs[:10]
    step = pl.program_id(0)
    head = meta[HEADS_AT + step]
    if slabs:
        near, away = refs[10:12]
        weights_in = refs[12 : 12 + 2 * slabs]
        dq, dko, dvo, low, high, kw, vw, dka, dva, gs = refs[-10:]
        per = gs.shape[0]
        for n in range(slabs):

            @pl.when(step == n * per)
            def _(n=n):
                made = dot(near[...], weights_in[2 * n][...], NT)
                made += dot(away[...], weights_in[2 * n + 1][...], NT)
                for m in range(per):
                    gs[m] = made[:, m * HEAD : (m + 1) * HEAD].astype(BF16)

        g = gs.at[lax.rem(step, per)]
    else:
        g = refs[10]
        dq, dko, dvo, low, high, kw, vw, dka, dva = refs[-9:]
    kw[0] = kb[0]
    kw[1] = ko[:TILE]
    kw[2] = ko[TILE:]
    kw[3] = ka[0]
    vw[0] = vb[0]
    vw[1] = vo[:TILE]
    vw[2] = vo[TILE:]
    vw[3] = va[0]
    dka[...] = jnp.zeros_like(dka)
    dva[...] = jnp.zeros_like(dva)
    ones = jnp.ones((16, HEAD), BF16)
    for t in range(2):
        rows = slice(t * TILE, (t + 1) * TILE)
        qt = q[rows, :]
        gt = g[rows, :]
        prod = gt.astype(F32) * o[rows, :].astype(F32)
        coarse = prod.astype(BF16)
        fine = (prod - coarse.astype(F32)).astype(BF16)
        delta = (dot(ones, coarse, NT) + dot(ones, fine, NT))[0:1]
        shift = norm[pl.ds(head, 1), rows] * LOG2E
        total = None
        for j in range(3):
            slot = meta[t * 3 + j]
            k = kw[slot]
            weights = jnp.exp2(dot(k, qt, NT) * (SCALE * LOG2E) - shift)
            score_grad = (weights * (dot(vw[slot], gt, NT) - delta)).astype(BF16)
            dva[slot] += dot(weights.astype(BF16), gt, NN)
            dka[slot] += dot(score_grad, qt, NN)
            part = dot(k, score_grad, TN)
            total = part if total is None else total + part
        dq[rows, :] = (total * SCALE).T.astype(BF16)
    dko[...] = dka[1:3].reshape(2 * TILE, HEAD)
    dvo[...] = dva[1:3].reshape(2 * TILE, HEAD)
    low[0] = dka[0].astype(BF16)
    low[1] = dva[0].astype(BF16)
    high[0] = dka[3].astype(BF16)
    high[1] = dva[3].astype(BF16)


def attend(meta, q, k, v, before, after, o, norm, g, slabs, grads, width, start, filled):
    heads = meta.shape[0] - HEADS_AT
    own = pl.BlockSpec((2 * TILE, HEAD), lambda i, m: (0, m[HEADS_AT + i]))
    rim_k = pl.BlockSpec((1, TILE, HEAD), lambda i, m: (0, 0, m[HEADS_AT + i]))
    rim_v = pl.BlockSpec((1, TILE, HEAD), lambda i, m: (1, 0, m[HEADS_AT + i]))
    local = pl.BlockSpec((2 * TILE, HEAD), lambda i, m: (0, i + start))
    local_rim = pl.BlockSpec((2, TILE, HEAD), lambda i, m: (0, 0, i + start))
    whole = pl.BlockSpec(norm.shape, lambda i, m: (0, 0))
    anywhere = pl.BlockSpec(memory_space=pl.ANY)
    wide = jax.ShapeDtypeStruct((2 * TILE, width), F32)
    rims = jax.ShapeDtypeStruct((2, TILE, width), BF16)
    in_specs = [own, rim_k, own, rim_k, rim_v, own, rim_v, own, whole]
    operands = [q, before, k, after, before, v, after, o, norm]
    scratch = [
        pltpu.VMEM((4, TILE, HEAD), BF16),
        pltpu.VMEM((4, TILE, HEAD), BF16),
        pltpu.VMEM((4, TILE, HEAD), F32),
        pltpu.VMEM((4, TILE, HEAD), F32),
    ]
    flops = heads * 6 * 5 * 2 * TILE * TILE * HEAD
    if slabs:
        rows, half = slabs[0][0].shape
        in_specs += [
            pl.BlockSpec((2 * TILE, half), lambda i, m: (0, m[6])),
            pl.BlockSpec((2 * TILE, half), lambda i, m: (0, 1 - m[6])),
        ]
        in_specs += [pl.BlockSpec((rows, half), lambda i, m: (0, 0))] * (2 * len(slabs))
        operands += [grads, grads, *(w for pair in slabs for w in pair)]
        scratch.append(pltpu.VMEM((rows // HEAD, 2 * TILE, HEAD), BF16))
        flops += heads * 2 * 2 * TILE * 2 * half * HEAD
    else:
        in_specs.append(pl.BlockSpec((2 * TILE, HEAD), lambda i, m: (0, i)))
        operands.append(g)
    return pl.pallas_call(
        functools.partial(attend_kernel, len(slabs)),
        grid_spec=pltpu.PrefetchScalarGridSpec(
            num_scalar_prefetch=1,
            grid=(heads,),
            in_specs=in_specs + [anywhere] * len(filled),
            out_specs=[own, local, local, local_rim, local_rim],
            scratch_shapes=scratch,
        ),
        out_shape=[jax.ShapeDtypeStruct(q.shape, BF16), wide, wide, rims, rims],
        input_output_aliases={1 + len(operands) + n: n for n in range(len(filled))},
        compiler_params=pltpu.CompilerParams(vmem_limit_bytes=VMEM),
        cost_estimate=pl.CostEstimate(
            flops=flops, bytes_accessed=heads * 2_000_000, transcendentals=heads * 6 * TILE * TILE
        ),
    )(meta, *operands, *filled)


def combine_kernel(edges, meta, *refs):
    dk, dv = refs[-2:]
    step = pl.program_id(0)
    for n, (start, stop) in enumerate(edges):
        dko, dvo, below, above = refs[4 * n : 4 * n + 4]

        @pl.when((step >= start) & (step < stop))
        def _(dko=dko, dvo=dvo, below=below, above=above):
            dk[:TILE] = ((dko[:TILE] + below[0].astype(F32)) * SCALE).astype(BF16)
            dk[TILE:] = ((dko[TILE:] + above[0].astype(F32)) * SCALE).astype(BF16)
            dv[:TILE] = (dvo[:TILE] + below[1].astype(F32)).astype(BF16)
            dv[TILE:] = (dvo[TILE:] + above[1].astype(F32)).astype(BF16)


def combine(blocks, groups, *filled):
    edges, in_specs, flat, start = [], [], [], 0
    wide = blocks[2]
    width = blocks[1] * wide
    anywhere = pl.BlockSpec(memory_space=pl.ANY)
    for group in groups:
        count = group[0].shape[1] // wide

        def at(i, start=start, count=count):
            return jnp.clip(i - start, 0, count - 1)

        own = pl.BlockSpec((2 * TILE, wide), lambda i, m, at=at: (0, at(i)))
        rim = pl.BlockSpec((2, TILE, wide), lambda i, m, at=at: (0, 0, at(i)))
        in_specs += [own, own, rim, rim]
        flat += group
        edges.append((start, start + count))
        start += count
    placed = pl.BlockSpec((2 * TILE, wide), lambda i, m: (0, m[i]))
    return pl.pallas_call(
        functools.partial(combine_kernel, edges),
        grid_spec=pltpu.PrefetchScalarGridSpec(
            num_scalar_prefetch=1,
            grid=(start,),
            in_specs=in_specs + [anywhere] * len(filled),
            out_specs=[placed, placed],
        ),
        out_shape=[jax.ShapeDtypeStruct((2 * TILE, width), BF16)] * 2,
        input_output_aliases={1 + len(flat) + n: n for n in range(len(filled))},
        compiler_params=pltpu.CompilerParams(vmem_limit_bytes=VMEM),
        cost_estimate=pl.CostEstimate(
            flops=4_000_000, bytes_accessed=20_000_000, transcendentals=0
        ),
    )(blocks[0], *flat, *filled)


def product_kernel(which, a, b, *refs):
    out = refs[-1]
    added = refs[:-1]
    zs, xs, ds, rows, columns = out.shape
    turned = a[...].T
    for half in range(xs // 2):
        wide = 2 * columns
        made = dot(turned, b[:, half * wide : (half + 1) * wide], NN)
        for d in range(ds):
            for z in range(zs):
                for n in range(2):
                    at = (d * zs + z) * rows
                    part = made[at : at + rows, n * columns : (n + 1) * columns]
                    if added:
                        part = part + added[half][z, n, d].astype(F32)
                    out[z, 2 * half + n, d] = part.astype(BF16)


def product(which, a, b, n_z, n_x, n_dp, parts, *added):
    tokens, width = a.shape
    wide = b.shape[1] // 2 // parts
    rows, columns = width // n_dp // n_z, b.shape[1] // 2 // n_x
    shape = (n_z, n_x // parts, n_dp, rows, columns)
    block = pl.BlockSpec((n_z, n_x // parts, 2, rows, columns), lambda i, m: (0, 0, i, 0, 0))
    piece = pl.BlockSpec((n_z, 2, 2, rows, columns), lambda i, m: (0, 0, i, 0, 0))
    return pl.pallas_call(
        product_kernel,
        grid_spec=pltpu.PrefetchScalarGridSpec(
            num_scalar_prefetch=1,
            grid=(n_dp // 2,),
            in_specs=[
                pl.BlockSpec((tokens, 2 * n_z * rows), lambda i, m: (0, i)),
                pl.BlockSpec((tokens, wide), lambda i, m: (0, m[0])),
            ]
            + [piece] * len(added),
            out_specs=block,
        ),
        out_shape=jax.ShapeDtypeStruct(shape, BF16),
        compiler_params=pltpu.CompilerParams(vmem_limit_bytes=VMEM),
        cost_estimate=pl.CostEstimate(
            flops=tokens * width * wide // 16, bytes_accessed=400_000, transcendentals=0
        ),
    )(which, a, b, *added)


def lay_kernel(pieces, out):
    n_x = pieces.shape[0] // 2
    columns = pieces.shape[2]
    for x in range(n_x):
        for c in range(2):
            at = (c * n_x + x) * columns
            out[:, at : at + columns] = pieces[2 * x + c].astype(F32)


def lay_out(pieces, n_z):
    count, rows, columns = pieces.shape
    wide = count // n_z * columns
    return pl.pallas_call(
        lay_kernel,
        grid=(n_z,),
        in_specs=[pl.BlockSpec((count // n_z, rows, columns), lambda i: (i, 0, 0))],
        out_specs=pl.BlockSpec((rows, wide), lambda i: (i, 0)),
        out_shape=jax.ShapeDtypeStruct((n_z * rows, wide), F32),
        compiler_params=pltpu.CompilerParams(vmem_limit_bytes=VMEM),
    )(pieces)


def pack_kernel(kf, kl, vf, vl, last, first):
    last[0] = kl[...]
    last[1] = vl[...]
    first[0] = kf[...]
    first[1] = vf[...]


def pack(k, v):
    steps = 3
    columns = k.shape[1] // steps
    end = k.shape[0] // TILE - 1
    head = pl.BlockSpec((TILE, columns), lambda i: (0, i))
    tail = pl.BlockSpec((TILE, columns), lambda i: (end, i))
    rim = pl.BlockSpec((2, TILE, columns), lambda i: (0, 0, i))
    shape = jax.ShapeDtypeStruct((2, TILE, k.shape[1]), BF16)
    return pl.pallas_call(
        pack_kernel,
        grid=(steps,),
        in_specs=[head, tail, head, tail],
        out_specs=[rim, rim],
        out_shape=[shape, shape],
        compiler_params=pltpu.CompilerParams(vmem_limit_bytes=VMEM),
    )(k, k, v, v)


def body(query, key_states, value_states, attn_out, log_norm, out_grad, out_weight, tile_lists):
    grad_rows = out_grad[0]
    out_rows = attn_out[0]
    q, k, v = query[0], key_states[0], value_states[0]
    norm = log_norm[0]
    tokens, width = q.shape
    model = grad_rows.shape[1]
    n_dp = lax.axis_size("dp")
    n_seq = lax.axis_size("seq")
    dp = lax.axis_index("dp")
    seq = lax.axis_index("seq")
    y = dp // 2
    core = seq % 2
    n_y = n_dp // 2
    n_x = 4
    n_z = n_seq // 2 // n_x

    def over_dp(value, target):
        return lax.ppermute(value, "dp", [(i, target(i)) for i in range(n_dp)])

    def over_seq(value, target):
        pairs = [(i, target(i)) for i in range(n_seq)]
        return lax.ppermute(value, "seq", [(i, j) for i, j in pairs if 0 <= j < n_seq])

    def swap(value):
        return over_seq(value, lambda i: i ^ 1)

    def up(value):
        return over_dp(value, lambda i: (i + 2) % n_dp)

    def down(value):
        return over_dp(value, lambda i: (i - 2) % n_dp)

    half = model // 2
    mine = lax.dynamic_slice_in_dim(out_weight, core * half, half, 1)
    last, first = pack(k, v)
    mine, last, first, left = lax.optimization_barrier((mine, last, first, out_rows))
    before = over_seq(last, lambda i: i + 1)
    after = over_seq(first, lambda i: i - 1)
    other = over_dp(mine, lambda i: i ^ 1)

    first_tile = seq * 2 - 1
    slots = (lax.dynamic_slice_in_dim(tile_lists[0], seq * 2, 2, 0) - first_tile).reshape(-1)

    send = 2 * (1 - core)
    sent0 = product(send[None], left, grad_rows, n_z, n_x, n_dp, 2)
    left, other = lax.optimization_barrier((left, other))
    sent1 = product((send + 1)[None], left, grad_rows, n_z, n_x, n_dp, 2)
    low_first = dp % 2 == 0
    pair0 = jnp.concatenate(
        [jnp.where(low_first, mine, other), jnp.where(low_first, other, mine)], axis=0
    )
    from_up = up(pair0)
    from_down = down(pair0)
    across0 = swap(pair0)
    rows_here = jnp.concatenate(
        [jnp.where(core == 0, pair0, across0), jnp.where(core == 0, across0, pair0)], axis=1
    )
    g0 = dot(grad_rows, rows_here, NT).astype(BF16)
    met0, met1, before, after, g0 = lax.optimization_barrier(
        (swap(sent0), swap(sent1), before, after, g0)
    )
    chip_sum = product(core[None], out_rows, grad_rows, n_z, n_x, n_dp, 1, met0, met1)
    chip_sum, g0 = lax.optimization_barrier((chip_sum, g0))
    chips = [[2 * i + c for i in range(n_seq // 2)] for c in range(2)]
    piece = chip_sum.shape[-2:]
    spread = lax.all_to_all(
        chip_sum.reshape(n_seq // 2, n_dp, *piece), "seq", 0, 0, axis_index_groups=chips
    )

    per = width // n_y // HEAD

    def attend_group(ats, g, slabs, width, start, filled):
        heads = [(at % n_y) * per + jnp.arange(per, dtype=jnp.int32) for at in ats]
        meta = jnp.concatenate([slots, core[None], *heads]).astype(jnp.int32)
        return attend(
            meta, q, k, v, before, after, out_rows, norm, g, slabs, grad_rows, width, start, filled
        )

    def rims_of(low, high):
        return [over_seq(high, lambda i: i + 1), over_seq(low, lambda i: i - 1)]

    three = width // n_y
    begun = attend_group([y], g0, [], 3 * three, 0, [])
    from_up, from_down, *begun = lax.optimization_barrier((from_up, from_down, *begun))
    far = up(from_up)
    across_up, across_down = swap(from_up), swap(from_down)
    most = attend_group(
        [y + n_y - 1, y + 1],
        None,
        [(from_up, across_up), (from_down, across_down)],
        3 * three,
        per,
        begun,
    )
    dq, dko, dvo, low, high = most
    spread, far, dq = lax.optimization_barrier((spread, far, dq))
    rims = rims_of(low, high)
    clip_sum = spread.astype(F32).sum(0).astype(BF16)
    dq, *rest = attend_group([y + 2], None, [(far, swap(far))], three, 0, [dq])
    pending = [[dko, dvo, *rims], [*rest[:2], *rims_of(*rest[2:])]]

    met = lax.all_to_all(clip_sum, "dp", 0, 0)
    met, dq, *rims = lax.optimization_barrier((met, dq, *pending[0][2:]))
    pending[0][2:] = rims
    total = met.astype(F32).sum(0).astype(BF16)
    ready = lax.all_to_all(jnp.broadcast_to(total, (n_seq, *piece)), "seq", 0, 0)
    weight_grad = lay_out(ready, n_z)

    blocks = jnp.stack([y, (y + n_y - 1) % n_y, (y + 1) % n_y, (y + 2) % n_y]).astype(jnp.int32)
    filled = combine((blocks[:3], n_y, three), pending[:1])
    dk, dv = combine((blocks[3:], n_y, three), pending[1:], *filled)
    return (dq[None], dk[None], dv[None], weight_grad)


def solution(mesh):
    placed = (
        P("dp", "seq", None),
        P("dp", "seq", None),
        P("dp", "seq", None),
        P("dp", "seq", None),
        P("dp", None, "seq"),
        P("dp", "seq", None),
        P("dp", None),
        P("dp", None, None),
    )
    return jax.shard_map(
        body,
        mesh=mesh,
        in_specs=placed,
        out_specs=(P("dp", "seq", None), P("dp", "seq", None), P("dp", "seq", None), P("dp", None)),
        check_vma=False,
    )
```

```python
import functools
import math

import jax
import jax.numpy as jnp
from jax import lax
from jax.experimental import pallas as pl
from jax.experimental.pallas import tpu as pltpu
from jax.sharding import PartitionSpec as P

TILE = 384
HEAD = 128
LOG2E = math.log2(math.e)
SCALE = 1.0 / math.sqrt(HEAD)
F32 = jnp.float32
BF16 = jnp.bfloat16
NT = (((1,), (1,)), ((), ()))
NN = (((1,), (0,)), ((), ()))
TN = (((0,), (0,)), ((), ()))


def dot(a, b, dims):
    return lax.dot_general(a, b, dims, preferred_element_type=F32)


HEADS_AT = 7
VMEM = 62 << 20


def attend_kernel(slabs, *refs):
    meta, q, kb, ko, ka, vb, vo, va, o, norm = refs[:10]
    step = pl.program_id(0)
    head = meta[HEADS_AT + step]
    if slabs:
        near, away = refs[10:12]
        weights_in = refs[12 : 12 + 2 * slabs]
        dq, dko, dvo, low, high, kw, vw, dka, dva, gs = refs[-10:]
        per = gs.shape[0]
        for n in range(slabs):

            @pl.when(step == n * per)
            def _(n=n):
                made = dot(near[...], weights_in[2 * n][...], NT)
                made += dot(away[...], weights_in[2 * n + 1][...], NT)
                for m in range(per):
                    gs[m] = made[:, m * HEAD : (m + 1) * HEAD].astype(BF16)

        g = gs.at[lax.rem(step, per)]
    else:
        g = refs[10]
        dq, dko, dvo, low, high, kw, vw, dka, dva = refs[-9:]
    kw[0] = kb[0]
    kw[1] = ko[:TILE]
    kw[2] = ko[TILE:]
    kw[3] = ka[0]
    vw[0] = vb[0]
    vw[1] = vo[:TILE]
    vw[2] = vo[TILE:]
    vw[3] = va[0]
    dka[...] = jnp.zeros_like(dka)
    dva[...] = jnp.zeros_like(dva)
    ones = jnp.ones((16, HEAD), BF16)
    for t in range(2):
        rows = slice(t * TILE, (t + 1) * TILE)
        qt = q[rows, :]
        gt = g[rows, :]
        prod = gt.astype(F32) * o[rows, :].astype(F32)
        coarse = prod.astype(BF16)
        fine = (prod - coarse.astype(F32)).astype(BF16)
        delta = (dot(ones, coarse, NT) + dot(ones, fine, NT))[0:1]
        shift = norm[pl.ds(head, 1), rows] * LOG2E
        total = None
        for j in range(3):
            slot = meta[t * 3 + j]
            k = kw[slot]
            weights = jnp.exp2(dot(k, qt, NT) * (SCALE * LOG2E) - shift)
            score_grad = (weights * (dot(vw[slot], gt, NT) - delta)).astype(BF16)
            dva[slot] += dot(weights.astype(BF16), gt, NN)
            dka[slot] += dot(score_grad, qt, NN)
            part = dot(k, score_grad, TN)
            total = part if total is None else total + part
        dq[rows, :] = (total * SCALE).T.astype(BF16)
    dko[...] = dka[1:3].reshape(2 * TILE, HEAD)
    dvo[...] = dva[1:3].reshape(2 * TILE, HEAD)
    low[0] = dka[0].astype(BF16)
    low[1] = dva[0].astype(BF16)
    high[0] = dka[3].astype(BF16)
    high[1] = dva[3].astype(BF16)


def attend(meta, q, k, v, before, after, o, norm, g, slabs, grads, width, start, filled):
    heads = meta.shape[0] - HEADS_AT
    own = pl.BlockSpec((2 * TILE, HEAD), lambda i, m: (0, m[HEADS_AT + i]))
    rim_k = pl.BlockSpec((1, TILE, HEAD), lambda i, m: (0, 0, m[HEADS_AT + i]))
    rim_v = pl.BlockSpec((1, TILE, HEAD), lambda i, m: (1, 0, m[HEADS_AT + i]))
    local = pl.BlockSpec((2 * TILE, HEAD), lambda i, m: (0, i + start))
    local_rim = pl.BlockSpec((2, TILE, HEAD), lambda i, m: (0, 0, i + start))
    whole = pl.BlockSpec(norm.shape, lambda i, m: (0, 0))
    anywhere = pl.BlockSpec(memory_space=pl.ANY)
    wide = jax.ShapeDtypeStruct((2 * TILE, width), F32)
    rims = jax.ShapeDtypeStruct((2, TILE, width), BF16)
    in_specs = [own, rim_k, own, rim_k, rim_v, own, rim_v, own, whole]
    operands = [q, before, k, after, before, v, after, o, norm]
    scratch = [
        pltpu.VMEM((4, TILE, HEAD), BF16),
        pltpu.VMEM((4, TILE, HEAD), BF16),
        pltpu.VMEM((4, TILE, HEAD), F32),
        pltpu.VMEM((4, TILE, HEAD), F32),
    ]
    flops = heads * 6 * 5 * 2 * TILE * TILE * HEAD
    if slabs:
        rows, half = slabs[0][0].shape
        in_specs += [
            pl.BlockSpec((2 * TILE, half), lambda i, m: (0, m[6])),
            pl.BlockSpec((2 * TILE, half), lambda i, m: (0, 1 - m[6])),
        ]
        in_specs += [pl.BlockSpec((rows, half), lambda i, m: (0, 0))] * (2 * len(slabs))
        operands += [grads, grads, *(w for pair in slabs for w in pair)]
        scratch.append(pltpu.VMEM((rows // HEAD, 2 * TILE, HEAD), BF16))
        flops += heads * 2 * 2 * TILE * 2 * half * HEAD
    else:
        in_specs.append(pl.BlockSpec((2 * TILE, HEAD), lambda i, m: (0, i)))
        operands.append(g)
    return pl.pallas_call(
        functools.partial(attend_kernel, len(slabs)),
        grid_spec=pltpu.PrefetchScalarGridSpec(
            num_scalar_prefetch=1,
            grid=(heads,),
            in_specs=in_specs + [anywhere] * len(filled),
            out_specs=[own, local, local, local_rim, local_rim],
            scratch_shapes=scratch,
        ),
        out_shape=[jax.ShapeDtypeStruct(q.shape, BF16), wide, wide, rims, rims],
        input_output_aliases={1 + len(operands) + n: n for n in range(len(filled))},
        compiler_params=pltpu.CompilerParams(vmem_limit_bytes=VMEM),
        cost_estimate=pl.CostEstimate(
            flops=flops, bytes_accessed=heads * 2_000_000, transcendentals=heads * 6 * TILE * TILE
        ),
    )(meta, *operands, *filled)


def combine_kernel(edges, meta, *refs):
    dk, dv = refs[-2:]
    step = pl.program_id(0)
    for n, (start, stop) in enumerate(edges):
        dko, dvo, below, above = refs[4 * n : 4 * n + 4]

        @pl.when((step >= start) & (step < stop))
        def _(dko=dko, dvo=dvo, below=below, above=above):
            dk[:TILE] = ((dko[:TILE] + below[0].astype(F32)) * SCALE).astype(BF16)
            dk[TILE:] = ((dko[TILE:] + above[0].astype(F32)) * SCALE).astype(BF16)
            dv[:TILE] = (dvo[:TILE] + below[1].astype(F32)).astype(BF16)
            dv[TILE:] = (dvo[TILE:] + above[1].astype(F32)).astype(BF16)


def combine(blocks, groups, *filled):
    edges, in_specs, flat, start = [], [], [], 0
    wide = blocks[2]
    width = blocks[1] * wide
    anywhere = pl.BlockSpec(memory_space=pl.ANY)
    for group in groups:
        count = group[0].shape[1] // wide

        def at(i, start=start, count=count):
            return jnp.clip(i - start, 0, count - 1)

        own = pl.BlockSpec((2 * TILE, wide), lambda i, m, at=at: (0, at(i)))
        rim = pl.BlockSpec((2, TILE, wide), lambda i, m, at=at: (0, 0, at(i)))
        in_specs += [own, own, rim, rim]
        flat += group
        edges.append((start, start + count))
        start += count
    placed = pl.BlockSpec((2 * TILE, wide), lambda i, m: (0, m[i]))
    return pl.pallas_call(
        functools.partial(combine_kernel, edges),
        grid_spec=pltpu.PrefetchScalarGridSpec(
            num_scalar_prefetch=1,
            grid=(start,),
            in_specs=in_specs + [anywhere] * len(filled),
            out_specs=[placed, placed],
        ),
        out_shape=[jax.ShapeDtypeStruct((2 * TILE, width), BF16)] * 2,
        input_output_aliases={1 + len(flat) + n: n for n in range(len(filled))},
        compiler_params=pltpu.CompilerParams(vmem_limit_bytes=VMEM),
        cost_estimate=pl.CostEstimate(
            flops=4_000_000, bytes_accessed=20_000_000, transcendentals=0
        ),
    )(blocks[0], *flat, *filled)


def product_kernel(which, a, b, *refs):
    out = refs[-1]
    added = refs[:-1]
    zs, xs, ds, rows, columns = out.shape
    turned = a[...].T
    for half in range(xs // 2):
        wide = 2 * columns
        made = dot(turned, b[:, half * wide : (half + 1) * wide], NN)
        for d in range(ds):
            for z in range(zs):
                for n in range(2):
                    at = (d * zs + z) * rows
                    part = made[at : at + rows, n * columns : (n + 1) * columns]
                    if added:
                        part = part + added[half][z, n, d].astype(F32)
                    out[z, 2 * half + n, d] = part.astype(BF16)


def product(which, a, b, n_z, n_x, n_dp, parts, *added):
    tokens, width = a.shape
    wide = b.shape[1] // 2 // parts
    rows, columns = width // n_dp // n_z, b.shape[1] // 2 // n_x
    shape = (n_z, n_x // parts, n_dp, rows, columns)
    block = pl.BlockSpec((n_z, n_x // parts, 2, rows, columns), lambda i, m: (0, 0, i, 0, 0))
    piece = pl.BlockSpec((n_z, 2, 2, rows, columns), lambda i, m: (0, 0, i, 0, 0))
    return pl.pallas_call(
        product_kernel,
        grid_spec=pltpu.PrefetchScalarGridSpec(
            num_scalar_prefetch=1,
            grid=(n_dp // 2,),
            in_specs=[
                pl.BlockSpec((tokens, 2 * n_z * rows), lambda i, m: (0, i)),
                pl.BlockSpec((tokens, wide), lambda i, m: (0, m[0])),
            ]
            + [piece] * len(added),
            out_specs=block,
        ),
        out_shape=jax.ShapeDtypeStruct(shape, BF16),
        compiler_params=pltpu.CompilerParams(vmem_limit_bytes=VMEM),
        cost_estimate=pl.CostEstimate(
            flops=tokens * width * wide // 16, bytes_accessed=400_000, transcendentals=0
        ),
    )(which, a, b, *added)


def lay_kernel(pieces, out):
    n_x = pieces.shape[0] // 2
    columns = pieces.shape[2]
    for x in range(n_x):
        for c in range(2):
            at = (c * n_x + x) * columns
            out[:, at : at + columns] = pieces[2 * x + c].astype(F32)


def lay_out(pieces, n_z):
    count, rows, columns = pieces.shape
    wide = count // n_z * columns
    return pl.pallas_call(
        lay_kernel,
        grid=(n_z,),
        in_specs=[pl.BlockSpec((count // n_z, rows, columns), lambda i: (i, 0, 0))],
        out_specs=pl.BlockSpec((rows, wide), lambda i: (i, 0)),
        out_shape=jax.ShapeDtypeStruct((n_z * rows, wide), F32),
        compiler_params=pltpu.CompilerParams(vmem_limit_bytes=VMEM),
    )(pieces)


def pack_kernel(kf, kl, vf, vl, last, first):
    last[0] = kl[...]
    last[1] = vl[...]
    first[0] = kf[...]
    first[1] = vf[...]


def pack(k, v):
    steps = 3
    columns = k.shape[1] // steps
    end = k.shape[0] // TILE - 1
    head = pl.BlockSpec((TILE, columns), lambda i: (0, i))
    tail = pl.BlockSpec((TILE, columns), lambda i: (end, i))
    rim = pl.BlockSpec((2, TILE, columns), lambda i: (0, 0, i))
    shape = jax.ShapeDtypeStruct((2, TILE, k.shape[1]), BF16)
    return pl.pallas_call(
        pack_kernel,
        grid=(steps,),
        in_specs=[head, tail, head, tail],
        out_specs=[rim, rim],
        out_shape=[shape, shape],
        compiler_params=pltpu.CompilerParams(vmem_limit_bytes=VMEM),
    )(k, k, v, v)


def body(query, key_states, value_states, attn_out, log_norm, out_grad, out_weight, tile_lists):
    grad_rows = out_grad[0]
    out_rows = attn_out[0]
    q, k, v = query[0], key_states[0], value_states[0]
    norm = log_norm[0]
    tokens, width = q.shape
    model = grad_rows.shape[1]
    n_dp = lax.axis_size("dp")
    n_seq = lax.axis_size("seq")
    dp = lax.axis_index("dp")
    seq = lax.axis_index("seq")
    y = dp // 2
    core = seq % 2
    n_y = n_dp // 2
    n_x = 4
    n_z = n_seq // 2 // n_x

    def over_dp(value, target):
        return lax.ppermute(value, "dp", [(i, target(i)) for i in range(n_dp)])

    def over_seq(value, target):
        pairs = [(i, target(i)) for i in range(n_seq)]
        return lax.ppermute(value, "seq", [(i, j) for i, j in pairs if 0 <= j < n_seq])

    def swap(value):
        return over_seq(value, lambda i: i ^ 1)

    def up(value):
        return over_dp(value, lambda i: (i + 2) % n_dp)

    def down(value):
        return over_dp(value, lambda i: (i - 2) % n_dp)

    half = model // 2
    mine = lax.dynamic_slice_in_dim(out_weight, core * half, half, 1)
    last, first = pack(k, v)
    mine, last, first, left = lax.optimization_barrier((mine, last, first, out_rows))
    before = over_seq(last, lambda i: i + 1)
    after = over_seq(first, lambda i: i - 1)
    other = over_dp(mine, lambda i: i ^ 1)

    first_tile = seq * 2 - 1
    slots = (lax.dynamic_slice_in_dim(tile_lists[0], seq * 2, 2, 0) - first_tile).reshape(-1)

    send = 2 * (1 - core)
    sent0 = product(send[None], left, grad_rows, n_z, n_x, n_dp, 2)
    left, other = lax.optimization_barrier((left, other))
    sent1 = product((send + 1)[None], left, grad_rows, n_z, n_x, n_dp, 2)
    low_first = dp % 2 == 0
    pair0 = jnp.concatenate(
        [jnp.where(low_first, mine, other), jnp.where(low_first, other, mine)], axis=0
    )
    from_up = up(pair0)
    from_down = down(pair0)
    across0 = swap(pair0)
    rows_here = jnp.concatenate(
        [jnp.where(core == 0, pair0, across0), jnp.where(core == 0, across0, pair0)], axis=1
    )
    g0 = dot(grad_rows, rows_here, NT).astype(BF16)
    met0, met1, before, after, g0 = lax.optimization_barrier(
        (swap(sent0), swap(sent1), before, after, g0)
    )
    chip_sum = product(core[None], out_rows, grad_rows, n_z, n_x, n_dp, 1, met0, met1)
    chip_sum, g0, from_up, from_down = lax.optimization_barrier((chip_sum, g0, from_up, from_down))
    chips = [[2 * i + c for i in range(n_seq // 2)] for c in range(2)]
    piece = chip_sum.shape[-2:]
    spread = lax.all_to_all(
        chip_sum.reshape(n_seq // 2, n_dp, *piece), "seq", 0, 0, axis_index_groups=chips
    )

    per = width // n_y // HEAD

    def attend_group(ats, g, slabs, width, start, filled):
        heads = [(at % n_y) * per + jnp.arange(per, dtype=jnp.int32) for at in ats]
        meta = jnp.concatenate([slots, core[None], *heads]).astype(jnp.int32)
        return attend(
            meta, q, k, v, before, after, out_rows, norm, g, slabs, grad_rows, width, start, filled
        )

    def rims_of(low, high):
        return [over_seq(high, lambda i: i + 1), over_seq(low, lambda i: i - 1)]

    three = width // n_y
    far = up(from_up)
    across_up, across_down = swap(from_up), swap(from_down)
    begun = attend_group([y], g0, [], 3 * three, 0, [])
    most = attend_group(
        [y + n_y - 1, y + 1],
        None,
        [(from_up, across_up), (from_down, across_down)],
        3 * three,
        per,
        begun,
    )
    dq, dko, dvo, low, high = most
    far, dq = lax.optimization_barrier((far, dq))
    rims = rims_of(low, high)
    dq, *rest = attend_group([y + 2], None, [(far, swap(far))], three, 0, [dq])
    pending = [[dko, dvo, *rims], [*rest[:2], *rims_of(*rest[2:])]]
    spread, dq = lax.optimization_barrier((spread, dq))
    clip_sum = spread.astype(F32).sum(0).astype(BF16)

    met = lax.all_to_all(clip_sum, "dp", 0, 0)
    met, *rims = lax.optimization_barrier((met, *pending[0][2:], *pending[1][2:]))
    pending[0][2:], pending[1][2:] = rims[:2], rims[2:]
    total = met.astype(F32).sum(0).astype(BF16)
    ready = lax.all_to_all(jnp.broadcast_to(total, (n_seq, *piece)), "seq", 0, 0)
    weight_grad = lay_out(ready, n_z)

    blocks = jnp.stack([y, (y + n_y - 1) % n_y, (y + 1) % n_y, (y + 2) % n_y]).astype(jnp.int32)
    filled = combine((blocks[:3], n_y, three), pending[:1])
    dk, dv = combine((blocks[3:], n_y, three), pending[1:], *filled)
    return (dq[None], dk[None], dv[None], weight_grad)


def solution(mesh):
    placed = (
        P("dp", "seq", None),
        P("dp", "seq", None),
        P("dp", "seq", None),
        P("dp", "seq", None),
        P("dp", None, "seq"),
        P("dp", "seq", None),
        P("dp", None),
        P("dp", None, None),
    )
    return jax.shard_map(
        body,
        mesh=mesh,
        in_specs=placed,
        out_specs=(P("dp", "seq", None), P("dp", "seq", None), P("dp", "seq", None), P("dp", None)),
        check_vma=False,
    )
```

```python
import functools
import math

import jax
import jax.numpy as jnp
from jax import lax
from jax.experimental import pallas as pl
from jax.experimental.pallas import tpu as pltpu
from jax.sharding import PartitionSpec as P

TILE = 384
HEAD = 128
LOG2E = math.log2(math.e)
SCALE = 1.0 / math.sqrt(HEAD)
F32 = jnp.float32
BF16 = jnp.bfloat16
NT = (((1,), (1,)), ((), ()))
NN = (((1,), (0,)), ((), ()))
TN = (((0,), (0,)), ((), ()))


def dot(a, b, dims):
    return lax.dot_general(a, b, dims, preferred_element_type=F32)


HEADS_AT = 7
VMEM = 62 << 20


def attend_kernel(slabs, *refs):
    meta, q, kb, ko, ka, vb, vo, va, o, norm = refs[:10]
    step = pl.program_id(0)
    head = meta[HEADS_AT + step]
    if slabs:
        near, away = refs[10:12]
        weights_in = refs[12 : 12 + 2 * slabs]
        dq, dko, dvo, low, high, kw, vw, dka, dva, gs = refs[-10:]
        per = gs.shape[0]
        for n in range(slabs):

            @pl.when(step == n * per)
            def _(n=n):
                made = dot(near[...], weights_in[2 * n][...], NT)
                made += dot(away[...], weights_in[2 * n + 1][...], NT)
                for m in range(per):
                    gs[m] = made[:, m * HEAD : (m + 1) * HEAD].astype(BF16)

        g = gs.at[lax.rem(step, per)]
    else:
        g = refs[10]
        dq, dko, dvo, low, high, kw, vw, dka, dva = refs[-9:]
    kw[0] = kb[0]
    kw[1] = ko[:TILE]
    kw[2] = ko[TILE:]
    kw[3] = ka[0]
    vw[0] = vb[0]
    vw[1] = vo[:TILE]
    vw[2] = vo[TILE:]
    vw[3] = va[0]
    dka[...] = jnp.zeros_like(dka)
    dva[...] = jnp.zeros_like(dva)
    ones = jnp.ones((16, HEAD), BF16)
    for t in range(2):
        rows = slice(t * TILE, (t + 1) * TILE)
        qt = q[rows, :]
        gt = g[rows, :]
        prod = gt.astype(F32) * o[rows, :].astype(F32)
        coarse = prod.astype(BF16)
        fine = (prod - coarse.astype(F32)).astype(BF16)
        delta = (dot(ones, coarse, NT) + dot(ones, fine, NT))[0:1]
        shift = norm[pl.ds(head, 1), rows] * LOG2E
        total = None
        for j in range(3):
            slot = meta[t * 3 + j]
            k = kw[slot]
            weights = jnp.exp2(dot(k, qt, NT) * (SCALE * LOG2E) - shift)
            score_grad = (weights * (dot(vw[slot], gt, NT) - delta)).astype(BF16)
            dva[slot] += dot(weights.astype(BF16), gt, NN)
            dka[slot] += dot(score_grad, qt, NN)
            part = dot(k, score_grad, TN)
            total = part if total is None else total + part
        dq[rows, :] = (total * SCALE).T.astype(BF16)
    dko[...] = dka[1:3].reshape(2 * TILE, HEAD)
    dvo[...] = dva[1:3].reshape(2 * TILE, HEAD)
    low[0] = dka[0].astype(BF16)
    low[1] = dva[0].astype(BF16)
    high[0] = dka[3].astype(BF16)
    high[1] = dva[3].astype(BF16)


def attend(meta, q, k, v, before, after, o, norm, g, slabs, grads, width, start, filled):
    heads = meta.shape[0] - HEADS_AT
    own = pl.BlockSpec((2 * TILE, HEAD), lambda i, m: (0, m[HEADS_AT + i]))
    rim_k = pl.BlockSpec((1, TILE, HEAD), lambda i, m: (0, 0, m[HEADS_AT + i]))
    rim_v = pl.BlockSpec((1, TILE, HEAD), lambda i, m: (1, 0, m[HEADS_AT + i]))
    local = pl.BlockSpec((2 * TILE, HEAD), lambda i, m: (0, i + start))
    local_rim = pl.BlockSpec((2, TILE, HEAD), lambda i, m: (0, 0, i + start))
    whole = pl.BlockSpec(norm.shape, lambda i, m: (0, 0))
    anywhere = pl.BlockSpec(memory_space=pl.ANY)
    wide = jax.ShapeDtypeStruct((2 * TILE, width), F32)
    rims = jax.ShapeDtypeStruct((2, TILE, width), BF16)
    in_specs = [own, rim_k, own, rim_k, rim_v, own, rim_v, own, whole]
    operands = [q, before, k, after, before, v, after, o, norm]
    scratch = [
        pltpu.VMEM((4, TILE, HEAD), BF16),
        pltpu.VMEM((4, TILE, HEAD), BF16),
        pltpu.VMEM((4, TILE, HEAD), F32),
        pltpu.VMEM((4, TILE, HEAD), F32),
    ]
    flops = heads * 6 * 5 * 2 * TILE * TILE * HEAD
    if slabs:
        rows, half = slabs[0][0].shape
        in_specs += [
            pl.BlockSpec((2 * TILE, half), lambda i, m: (0, m[6])),
            pl.BlockSpec((2 * TILE, half), lambda i, m: (0, 1 - m[6])),
        ]
        in_specs += [pl.BlockSpec((rows, half), lambda i, m: (0, 0))] * (2 * len(slabs))
        operands += [grads, grads, *(w for pair in slabs for w in pair)]
        scratch.append(pltpu.VMEM((rows // HEAD, 2 * TILE, HEAD), BF16))
        flops += heads * 2 * 2 * TILE * 2 * half * HEAD
    else:
        in_specs.append(pl.BlockSpec((2 * TILE, HEAD), lambda i, m: (0, i)))
        operands.append(g)
    return pl.pallas_call(
        functools.partial(attend_kernel, len(slabs)),
        grid_spec=pltpu.PrefetchScalarGridSpec(
            num_scalar_prefetch=1,
            grid=(heads,),
            in_specs=in_specs + [anywhere] * len(filled),
            out_specs=[own, local, local, local_rim, local_rim],
            scratch_shapes=scratch,
        ),
        out_shape=[jax.ShapeDtypeStruct(q.shape, BF16), wide, wide, rims, rims],
        input_output_aliases={1 + len(operands) + n: n for n in range(len(filled))},
        compiler_params=pltpu.CompilerParams(vmem_limit_bytes=VMEM),
        cost_estimate=pl.CostEstimate(
            flops=flops, bytes_accessed=heads * 2_000_000, transcendentals=heads * 6 * TILE * TILE
        ),
    )(meta, *operands, *filled)


def combine_kernel(edges, meta, *refs):
    dk, dv = refs[-2:]
    step = pl.program_id(0)
    for n, (start, stop) in enumerate(edges):
        dko, dvo, below, above = refs[4 * n : 4 * n + 4]

        @pl.when((step >= start) & (step < stop))
        def _(dko=dko, dvo=dvo, below=below, above=above):
            dk[:TILE] = ((dko[:TILE] + below[0].astype(F32)) * SCALE).astype(BF16)
            dk[TILE:] = ((dko[TILE:] + above[0].astype(F32)) * SCALE).astype(BF16)
            dv[:TILE] = (dvo[:TILE] + below[1].astype(F32)).astype(BF16)
            dv[TILE:] = (dvo[TILE:] + above[1].astype(F32)).astype(BF16)


def combine(blocks, groups, *filled):
    edges, in_specs, flat, start = [], [], [], 0
    wide = blocks[2]
    width = blocks[1] * wide
    anywhere = pl.BlockSpec(memory_space=pl.ANY)
    for group in groups:
        count = group[0].shape[1] // wide

        def at(i, start=start, count=count):
            return jnp.clip(i - start, 0, count - 1)

        own = pl.BlockSpec((2 * TILE, wide), lambda i, m, at=at: (0, at(i)))
        rim = pl.BlockSpec((2, TILE, wide), lambda i, m, at=at: (0, 0, at(i)))
        in_specs += [own, own, rim, rim]
        flat += group
        edges.append((start, start + count))
        start += count
    placed = pl.BlockSpec((2 * TILE, wide), lambda i, m: (0, m[i]))
    return pl.pallas_call(
        functools.partial(combine_kernel, edges),
        grid_spec=pltpu.PrefetchScalarGridSpec(
            num_scalar_prefetch=1,
            grid=(start,),
            in_specs=in_specs + [anywhere] * len(filled),
            out_specs=[placed, placed],
        ),
        out_shape=[jax.ShapeDtypeStruct((2 * TILE, width), BF16)] * 2,
        input_output_aliases={1 + len(flat) + n: n for n in range(len(filled))},
        compiler_params=pltpu.CompilerParams(vmem_limit_bytes=VMEM),
        cost_estimate=pl.CostEstimate(
            flops=4_000_000, bytes_accessed=20_000_000, transcendentals=0
        ),
    )(blocks[0], *flat, *filled)


def product_kernel(which, a, b, *refs):
    out = refs[-1]
    added = refs[:-1]
    zs, xs, ds, rows, columns = out.shape
    turned = a[...].T
    for half in range(xs // 2):
        wide = 2 * columns
        made = dot(turned, b[:, half * wide : (half + 1) * wide], NN)
        for d in range(ds):
            for z in range(zs):
                for n in range(2):
                    at = (d * zs + z) * rows
                    part = made[at : at + rows, n * columns : (n + 1) * columns]
                    if added:
                        part = part + added[half][z, n, d].astype(F32)
                    out[z, 2 * half + n, d] = part.astype(BF16)


def product(which, a, b, n_z, n_x, n_dp, parts, *added):
    tokens, width = a.shape
    wide = b.shape[1] // 2 // parts
    rows, columns = width // n_dp // n_z, b.shape[1] // 2 // n_x
    shape = (n_z, n_x // parts, n_dp, rows, columns)
    block = pl.BlockSpec((n_z, n_x // parts, 2, rows, columns), lambda i, m: (0, 0, i, 0, 0))
    piece = pl.BlockSpec((n_z, 2, 2, rows, columns), lambda i, m: (0, 0, i, 0, 0))
    return pl.pallas_call(
        product_kernel,
        grid_spec=pltpu.PrefetchScalarGridSpec(
            num_scalar_prefetch=1,
            grid=(n_dp // 2,),
            in_specs=[
                pl.BlockSpec((tokens, 2 * n_z * rows), lambda i, m: (0, i)),
                pl.BlockSpec((tokens, wide), lambda i, m: (0, m[0])),
            ]
            + [piece] * len(added),
            out_specs=block,
        ),
        out_shape=jax.ShapeDtypeStruct(shape, BF16),
        compiler_params=pltpu.CompilerParams(vmem_limit_bytes=VMEM),
        cost_estimate=pl.CostEstimate(
            flops=tokens * width * wide // 16, bytes_accessed=400_000, transcendentals=0
        ),
    )(which, a, b, *added)


def lay_kernel(pieces, out):
    n_x = pieces.shape[0] // 2
    columns = pieces.shape[2]
    for x in range(n_x):
        for c in range(2):
            at = (c * n_x + x) * columns
            out[:, at : at + columns] = pieces[2 * x + c].astype(F32)


def lay_out(pieces, n_z):
    count, rows, columns = pieces.shape
    wide = count // n_z * columns
    return pl.pallas_call(
        lay_kernel,
        grid=(n_z,),
        in_specs=[pl.BlockSpec((count // n_z, rows, columns), lambda i: (i, 0, 0))],
        out_specs=pl.BlockSpec((rows, wide), lambda i: (i, 0)),
        out_shape=jax.ShapeDtypeStruct((n_z * rows, wide), F32),
        compiler_params=pltpu.CompilerParams(vmem_limit_bytes=VMEM),
    )(pieces)


def pack_kernel(kf, kl, vf, vl, last, first):
    last[0] = kl[...]
    last[1] = vl[...]
    first[0] = kf[...]
    first[1] = vf[...]


def pack(k, v):
    steps = 3
    columns = k.shape[1] // steps
    end = k.shape[0] // TILE - 1
    head = pl.BlockSpec((TILE, columns), lambda i: (0, i))
    tail = pl.BlockSpec((TILE, columns), lambda i: (end, i))
    rim = pl.BlockSpec((2, TILE, columns), lambda i: (0, 0, i))
    shape = jax.ShapeDtypeStruct((2, TILE, k.shape[1]), BF16)
    return pl.pallas_call(
        pack_kernel,
        grid=(steps,),
        in_specs=[head, tail, head, tail],
        out_specs=[rim, rim],
        out_shape=[shape, shape],
        compiler_params=pltpu.CompilerParams(vmem_limit_bytes=VMEM),
    )(k, k, v, v)


def body(query, key_states, value_states, attn_out, log_norm, out_grad, out_weight, tile_lists):
    grad_rows = out_grad[0]
    out_rows = attn_out[0]
    q, k, v = query[0], key_states[0], value_states[0]
    norm = log_norm[0]
    tokens, width = q.shape
    model = grad_rows.shape[1]
    n_dp = lax.axis_size("dp")
    n_seq = lax.axis_size("seq")
    dp = lax.axis_index("dp")
    seq = lax.axis_index("seq")
    y = dp // 2
    core = seq % 2
    n_y = n_dp // 2
    n_x = 4
    n_z = n_seq // 2 // n_x

    def over_dp(value, target):
        return lax.ppermute(value, "dp", [(i, target(i)) for i in range(n_dp)])

    def over_seq(value, target):
        pairs = [(i, target(i)) for i in range(n_seq)]
        return lax.ppermute(value, "seq", [(i, j) for i, j in pairs if 0 <= j < n_seq])

    def swap(value):
        return over_seq(value, lambda i: i ^ 1)

    def up(value):
        return over_dp(value, lambda i: (i + 2) % n_dp)

    def down(value):
        return over_dp(value, lambda i: (i - 2) % n_dp)

    half = model // 2
    mine = lax.dynamic_slice_in_dim(out_weight, core * half, half, 1)
    last, first = pack(k, v)
    mine, last, first, left = lax.optimization_barrier((mine, last, first, out_rows))
    before = over_seq(last, lambda i: i + 1)
    after = over_seq(first, lambda i: i - 1)
    other = over_dp(mine, lambda i: i ^ 1)

    first_tile = seq * 2 - 1
    slots = (lax.dynamic_slice_in_dim(tile_lists[0], seq * 2, 2, 0) - first_tile).reshape(-1)

    send = 2 * (1 - core)
    sent0 = product(send[None], left, grad_rows, n_z, n_x, n_dp, 2)
    left, other = lax.optimization_barrier((left, other))
    sent1 = product((send + 1)[None], left, grad_rows, n_z, n_x, n_dp, 2)
    low_first = dp % 2 == 0
    pair0 = jnp.concatenate(
        [jnp.where(low_first, mine, other), jnp.where(low_first, other, mine)], axis=0
    )
    from_up = up(pair0)
    from_down = down(pair0)
    across0 = swap(pair0)
    rows_here = jnp.concatenate(
        [jnp.where(core == 0, pair0, across0), jnp.where(core == 0, across0, pair0)], axis=1
    )
    g0 = dot(grad_rows, rows_here, NT).astype(BF16)
    met0, met1, before, after, g0 = lax.optimization_barrier(
        (swap(sent0), swap(sent1), before, after, g0)
    )
    chip_sum = product(core[None], out_rows, grad_rows, n_z, n_x, n_dp, 1, met0, met1)
    chip_sum, g0, from_up, from_down = lax.optimization_barrier((chip_sum, g0, from_up, from_down))
    chips = [[2 * i + c for i in range(n_seq // 2)] for c in range(2)]
    piece = chip_sum.shape[-2:]
    spread = lax.all_to_all(
        chip_sum.reshape(n_seq // 2, n_dp, *piece), "seq", 0, 0, axis_index_groups=chips
    )

    per = width // n_y // HEAD

    def attend_group(ats, g, slabs, width, start, filled):
        heads = [(at % n_y) * per + jnp.arange(per, dtype=jnp.int32) for at in ats]
        meta = jnp.concatenate([slots, core[None], *heads]).astype(jnp.int32)
        return attend(
            meta, q, k, v, before, after, out_rows, norm, g, slabs, grad_rows, width, start, filled
        )

    def rims_of(low, high):
        return [over_seq(high, lambda i: i + 1), over_seq(low, lambda i: i - 1)]

    three = width // n_y
    far = up(from_up)
    across_up, across_down = swap(from_up), swap(from_down)
    begun = attend_group([y], g0, [], 3 * three, 0, [])
    most = attend_group(
        [y + n_y - 1, y + 1],
        None,
        [(from_up, across_up), (from_down, across_down)],
        3 * three,
        per,
        begun,
    )
    dq, dko, dvo, low, high = most
    far, dq = lax.optimization_barrier((far, dq))
    rims = rims_of(low, high)
    dq, *rest = attend_group([y + 2], None, [(far, swap(far))], three, 0, [dq])
    spread, dq = lax.optimization_barrier((spread, dq))
    clip_sum = spread.astype(F32).sum(0).astype(BF16)
    clip_sum, *edges = lax.optimization_barrier((clip_sum, *rest[2:]))
    pending = [[dko, dvo, *rims], [*rest[:2], *rims_of(*edges)]]

    met = lax.all_to_all(clip_sum, "dp", 0, 0)
    met, *rims = lax.optimization_barrier((met, *pending[0][2:], *pending[1][2:]))
    pending[0][2:], pending[1][2:] = rims[:2], rims[2:]
    total = met.astype(F32).sum(0).astype(BF16)
    ready = lax.all_to_all(jnp.broadcast_to(total, (n_seq, *piece)), "seq", 0, 0)
    weight_grad = lay_out(ready, n_z)

    blocks = jnp.stack([y, (y + n_y - 1) % n_y, (y + 1) % n_y, (y + 2) % n_y]).astype(jnp.int32)
    filled = combine((blocks[:3], n_y, three), pending[:1])
    dk, dv = combine((blocks[3:], n_y, three), pending[1:], *filled)
    return (dq[None], dk[None], dv[None], weight_grad)


def solution(mesh):
    placed = (
        P("dp", "seq", None),
        P("dp", "seq", None),
        P("dp", "seq", None),
        P("dp", "seq", None),
        P("dp", None, "seq"),
        P("dp", "seq", None),
        P("dp", None),
        P("dp", None, None),
    )
    return jax.shard_map(
        body,
        mesh=mesh,
        in_specs=placed,
        out_specs=(P("dp", "seq", None), P("dp", "seq", None), P("dp", "seq", None), P("dp", None)),
        check_vma=False,
    )
```
